32 devices in a mesh: dp: 32 (over z, y, x, core).
Axes of the slice: x: 2, y: 2, z: 4, core: 2. Of those that a mesh axis runs over, the one named last changes fastest.
Arguments:
- queries: bfloat16 [4096, 768], P('dp'), may hold values from -2 to 2
- documents: bfloat16 [4096, 768], P('dp'), may hold values from -2 to 2
- positives: int32 [4096], P('dp'), may hold values from 0 to 4095, each once
Outputs:
- loss: float32 [], replicated
- grad_queries: float32 [4096, 768], P('dp')
- grad_documents: float32 [4096, 768], P('dp')
The draws below stay inside these ranges and needn't reach their ends.
Inputs may be any that keep to these rules, and one draw needn't show every extreme that they name: `positives`: every document is the positive of exactly one query.
All inputs are finite; a program needn't handle non-finite values.
Results may differ from the reference program's by a relative error of at most 0.0004.
The reference program's roundings to bfloat16 on the way (of `qb` and `weights`) count: a program that leaves them out, or rounds other values in their place, can miss the bound.
Values may be sent and summed in bfloat16 or wider, within the bound.
A program may use at most 192 MiB of HBM per device.

```python
import math
import jax
import jax.numpy as jnp
from jax import lax

D = 768
QUERIES = 4096
DOCS = 4096


def row_scales(key, count):
    return jnp.exp(jax.random.uniform(key, (count, 1), jnp.float32, math.log(0.3), math.log(3.0)))


def draw_queries(key, part):
    key = jax.random.fold_in(key, 11)
    key_scale, key_body = jax.random.split(key)
    scales = row_scales(key_scale, QUERIES)
    values = jnp.clip(jax.random.normal(key_body, (QUERIES, D), jnp.float32), -4.0, 4.0)
    return (scales * values / math.sqrt(D)).astype(jnp.bfloat16)


def draw_documents(key, part):
    key = jax.random.fold_in(key, 23)
    key_scale, key_body = jax.random.split(key)
    scales = row_scales(key_scale, DOCS)
    values = jnp.clip(jax.random.normal(key_body, (DOCS, D), jnp.float32), -4.0, 4.0)
    return (scales * values / math.sqrt(D)).astype(jnp.bfloat16)


def setup_inputs(seed: int = 0) -> dict:
    key_of = jax.random.split(jax.random.key(seed), 4)
    queries = draw_queries(jax.random.fold_in(key_of[3], 71), 0)
    documents = draw_documents(jax.random.fold_in(key_of[3], 71), 0)
    positives = jax.random.permutation(key_of[2], QUERIES).astype(jnp.int32)
    return {"queries": queries, "documents": documents, "positives": positives}


def normalize(values):
    wide = values.astype(jnp.float32)
    length = jnp.sqrt(lax.optimization_barrier(jnp.sum(wide * wide, axis=1, keepdims=True)) + 1e-06)
    return (wide / length, length)

def reference(queries, documents, positives):
    qn, qnorm = normalize(queries)
    dn, dnorm = normalize(documents)
    qb = qn.astype(jnp.bfloat16)
    db = dn.astype(jnp.bfloat16)
    block = math.gcd(QUERIES, 512)
    qblocks = qb.reshape(QUERIES // block, block, D)
    pblocks = positives.reshape(QUERIES // block, block)
    columns = jnp.arange(DOCS, dtype=jnp.int32)

    def per_block(carry, item):
        loss_sum, grad_docs = carry
        rows, picks = item
        scores = 20.0 * jnp.dot(rows, db.T, preferred_element_type=jnp.float32)
        lse = 20.0 + jnp.log(lax.optimization_barrier(jnp.sum(jnp.exp(scores - 20.0), axis=1)))
        hit = picks[:, None] == columns[None, :]
        positive_score = lax.optimization_barrier(jnp.sum(jnp.where(hit, scores, jnp.float32(0.0)), axis=1))
        weights = (jnp.exp(scores - lse[:, None]) - hit.astype(jnp.float32)).astype(jnp.bfloat16)
        grad_rows = 20.0 * jnp.dot(weights, db, preferred_element_type=jnp.float32)
        grad_docs = grad_docs + 20.0 * jnp.dot(weights.T, rows, preferred_element_type=jnp.float32)
        return ((loss_sum + jnp.sum(lse - positive_score), grad_docs), grad_rows)
    start = (jnp.zeros((), jnp.float32), jnp.zeros((DOCS, D), jnp.float32))
    (loss_sum, gd), stacked = lax.scan(per_block, start, (qblocks, pblocks))
    gq = stacked.reshape(QUERIES, D)
    grad_queries = (gq - lax.optimization_barrier(jnp.sum(gq * qn, axis=1, keepdims=True)) * qn) / qnorm
    grad_documents = (gd - lax.optimization_barrier(jnp.sum(gd * dn, axis=1, keepdims=True)) * dn) / dnorm
    return (loss_sum / QUERIES, grad_queries, grad_documents)
```

```python
import functools

import jax
import jax.numpy as jnp
from jax import lax
from jax.experimental import pallas as pl
from jax.experimental.pallas import tpu as pltpu
from jax.sharding import PartitionSpec as P

PIECES = 2
F32 = jnp.float32
BF16 = jnp.bfloat16


def tree_sum(terms):
    while len(terms) > 1:
        terms = [terms[i] + terms[i + 1] for i in range(0, len(terms), 2)]
    return terms[0]


def normalize(values):
    wide = values.astype(F32)
    length = jnp.sqrt(jnp.sum(wide * wide, axis=1, keepdims=True) + 1e-06)
    return wide / length, length


def project(grad, unit, length):
    return (grad - jnp.sum(grad * unit, axis=1, keepdims=True) * unit) / length


def group_bits(n):
    bits = n.bit_length() - 1
    odd = [b for b in range(bits - 1, 0, -1) if b % 2 == 1]
    even = [b for b in range(bits - 1, 0, -1) if b % 2 == 0]
    return odd + [0], even


def kernel(
    n, qbits, dbits,
    q_ref, d_ref, pos_ref,
    loss_ref, outq_ref, outd_ref,
    qall, dall, posrow, expd, wts, stats, losses, accq, accd, gotq, gotd,
    qs_sem, qr_sem, ds_sem, dr_sem, ps_sem, pr_sem, ss_sem, sr_sem, ls_sem, lr_sem,
    aqs_sem, aqr_sem, ads_sem, adr_sem,
):
    me = lax.axis_index("dp")
    c = q_ref.shape[0]
    piece = c // PIECES
    nq, nd = 1 << len(qbits), 1 << len(dbits)
    rows_q, rows_d = nq * c, nd * c

    def flipped(bits, slot):
        where = me
        for j, b in enumerate(bits):
            if (slot >> j) & 1:
                where = where + (1 - 2 * (lax.rem(lax.div(me, 1 << b), 2))) * (1 << b)
        return where

    peer_q = [flipped(qbits, k) for k in range(nq)]
    peer_d = [flipped(dbits, k) for k in range(nd)]

    barrier = pltpu.get_barrier_semaphore()
    for peer in peer_q[1:] + peer_d[1:]:
        pl.semaphore_signal(barrier, inc=1, device_id=(peer,), device_id_type=pl.DeviceIdType.MESH)

    qn, qnorm = normalize(q_ref[...])
    dn, dnorm = normalize(d_ref[...])
    qall[pl.ds(0, c), :] = qn.astype(BF16)
    dall[pl.ds(0, c), :] = dn.astype(BF16)
    posrow[:, pl.ds(0, c)] = pos_ref[...]

    pl.semaphore_wait(barrier, nq + nd - 2)

    def remote(src, dst, send, recv, peer):
        return pltpu.make_async_remote_copy(
            src_ref=src, dst_ref=dst, send_sem=send, recv_sem=recv,
            device_id=(peer,), device_id_type=pl.DeviceIdType.MESH,
        )

    def stage_of(slot):
        return slot.bit_length() - 1

    def gather_copy(buf, send, recv, peers, slot, p):
        low = slot - (1 << stage_of(slot))
        return remote(
            buf.at[pl.ds(low * c + p * piece, piece), :],
            buf.at[pl.ds(slot * c + p * piece, piece), :],
            send.at[slot, p], recv.at[slot, p], peers[1 << stage_of(slot)],
        )

    gq = functools.partial(gather_copy, qall, qs_sem, qr_sem, peer_q)
    gd = functools.partial(gather_copy, dall, ds_sem, dr_sem, peer_d)
    pos_copies = [
        remote(posrow.at[:, pl.ds(0, c)], posrow.at[:, pl.ds(k * c, c)],
               ps_sem.at[k], pr_sem.at[k], peer_q[k])
        for k in range(1, nq)
    ]

    for p in range(PIECES):
        for j in range(max(len(qbits), len(dbits))):
            if j < len(dbits):
                gd(1 << j, p).start()
            if j < len(qbits):
                gq(1 << j, p).start()
    for copy in pos_copies:
        copy.start()

    def arrive(make, bits, slot, p):
        make(slot, p).wait_recv()
        for j in range(stage_of(slot) + 1, len(bits)):
            make(slot + (1 << j), p).start()

    half = nq // 2
    for slot in range(1, max(half, nd)):
        for p in range(PIECES):
            if slot < half:
                arrive(gq, qbits, slot, p)
            if slot < nd:
                arrive(gd, dbits, slot, p)
    for copy in pos_copies:
        copy.wait_recv()

    pair = 2 * c
    bases = [peer_d[r] * c for r in range(nd)]

    def hits(j, r):
        here = posrow[:, pl.ds(pl.multiple_of(j * pair, pair), pair)] - bases[r]
        return lax.broadcasted_iota(jnp.int32, (c, pair), 0) == here

    def score_pair(j, carry):
        lanes = pl.ds(pl.multiple_of(j * pair, pair), pair)
        total = jnp.zeros((1, pair), F32)
        picked = jnp.zeros((1, pair), F32)
        dots = lax.dot_general(
            dall[...], qall[lanes, :], (((1,), (1,)), ((), ())), preferred_element_type=F32
        )
        for r in range(nd):
            scores = 20.0 * dots[r * c:(r + 1) * c, :]
            powers = jnp.exp(scores - 20.0)
            expd[pl.ds(r * c, c), lanes] = powers
            total = total + jnp.sum(powers, axis=0, keepdims=True)
            picked = picked + jnp.sum(jnp.where(hits(j, r), scores, 0.0), axis=0, keepdims=True)
        stats[0, 0:1, lanes] = total
        stats[0, 1:2, lanes] = picked
        return carry

    lax.fori_loop(0, nq // 4, score_pair, 0)
    for slot in range(half, nq):
        for p in range(PIECES):
            gq(slot, p).wait_recv()
    lax.fori_loop(nq // 4, nq // 2, score_pair, 0)

    stat_copies = [
        remote(stats.at[0], stats.at[k], ss_sem.at[k], sr_sem.at[k], peer_q[k])
        for k in range(1, nq)
    ]
    for copy in stat_copies:
        copy.start()
    for copy in stat_copies:
        copy.wait_recv()

    def slot_total(row, r):
        return tree_sum([stats[k, row:row + 1, pl.ds((r ^ k) * c, c)] for k in range(nq)])

    totals = [slot_total(0, r) for r in range(nq)]
    losses[0] = tree_sum([20.0 + jnp.log(totals[r]) - slot_total(1, r) for r in range(nq)])
    loss_copies = [
        remote(losses.at[0], losses.at[k], ls_sem.at[k], lr_sem.at[k], peer_d[k])
        for k in range(1, nd)
    ]

    for j in range(nq // 2):
        inverse = 1.0 / jnp.concatenate([totals[2 * j], totals[2 * j + 1]], axis=1)
        lanes = pl.ds(j * pair, pair)
        for r in range(nd):
            rows = pl.ds(r * c, c)
            hit = jnp.where(hits(j, r), 1.0, 0.0)
            wts[rows, lanes] = (expd[rows, lanes] * inverse - hit).astype(BF16)

    def reduce_copy(acc, got, send, recv, peers, slot, p):
        rows = pl.ds(slot * c + p * piece, piece)
        return remote(acc.at[rows, :], got.at[rows, :], send.at[slot, p], recv.at[slot, p],
                      peers[1 << stage_of(slot)])

    rq = functools.partial(reduce_copy, accq, gotq, aqs_sem, aqr_sem, peer_q)
    rd = functools.partial(reduce_copy, accd, gotd, ads_sem, adr_sem, peer_d)

    def grad_q(j):
        rows = pl.ds(j * pair, pair)
        accq[rows, :] = lax.dot_general(
            wts[:, rows], dall[...], (((0,), (0,)), ((), ())), preferred_element_type=F32
        )
        if 2 * j >= nq // 2:
            for slot in (2 * j + 1, 2 * j):
                for p in range(PIECES):
                    rq(slot, p).start()

    def grad_d(j):
        rows = pl.ds(j * pair, pair)
        accd[rows, :] = jnp.dot(wts[rows, :], qall[...], preferred_element_type=F32)
        if 2 * j >= nd // 2:
            for slot in (2 * j + 1, 2 * j):
                for p in range(PIECES):
                    rd(slot, p).start()

    pairs_q, pairs_d = nq // 2, nd // 2
    for j in reversed(range(pairs_d // 2, pairs_d)):
        grad_d(j)
    for j in reversed(range(3 * pairs_q // 4, pairs_q)):
        grad_q(j)
    for j in reversed(range(pairs_q // 4, pairs_q // 2)):
        grad_q(j)
    for j in reversed(range(pairs_q // 2, 3 * pairs_q // 4)):
        grad_q(j)
    for j in reversed(range(pairs_q // 4)):
        grad_q(j)
    for j in reversed(range(pairs_d // 2)):
        grad_d(j)
    for copy in loss_copies:
        copy.start()

    def absorb(make, acc, got, slot, p):
        make(slot, p).wait_recv()
        into = slot - (1 << stage_of(slot))
        rows = pl.ds(into * c + p * piece, piece)
        acc[rows, :] = acc[rows, :] + got[pl.ds(slot * c + p * piece, piece), :]
        if into and stage_of(slot) == stage_of(into) + 1:
            make(into, p).start()

    def falling(high, low):
        return list(range(high - 1, low - 1, -1))

    order = [("q", t) for t in falling(nq, 3 * nq // 4)]
    order += [("d", t) for t in falling(nd, 3 * nd // 4)]
    order += [("q", t) for t in falling(3 * nq // 4, nq // 2)]
    rest_q, rest_d = falling(nq // 2, 1), falling(3 * nd // 4, 1)
    for i in range(max(len(rest_q), len(rest_d))):
        if i < len(rest_q):
            order.append(("q", rest_q[i]))
        if i < len(rest_d):
            order.append(("d", rest_d[i]))
    for which, slot in order:
        for p in range(PIECES):
            if which == "q":
                absorb(rq, accq, gotq, slot, p)
            else:
                absorb(rd, accd, gotd, slot, p)

    qn, qnorm = normalize(q_ref[...])
    outq_ref[...] = project(20.0 * accq[pl.ds(0, c), :], qn, qnorm)
    dn, dnorm = normalize(d_ref[...])
    outd_ref[...] = project(20.0 * accd[pl.ds(0, c), :], dn, dnorm)

    for copy in loss_copies:
        copy.wait_recv()
    row = tree_sum([losses[k] for k in range(nd)])
    loss_ref[...] = jnp.sum(row, axis=1, keepdims=True) / (c * n)

    for slot in range(1, nq):
        for p in range(PIECES):
            gq(slot, p).wait_send()
            rq(slot, p).wait_send()
    for slot in range(1, nd):
        for p in range(PIECES):
            gd(slot, p).wait_send()
            rd(slot, p).wait_send()
    for copy in pos_copies + stat_copies + loss_copies:
        copy.wait_send()


def local(queries, documents, positives):
    n = lax.axis_size("dp")
    c, width = queries.shape
    qbits, dbits = group_bits(n)
    nq, nd = 1 << len(qbits), 1 << len(dbits)
    dma = pltpu.SemaphoreType.DMA
    vmem = pl.BlockSpec(memory_space=pltpu.VMEM)
    loss, grad_q, grad_d = pl.pallas_call(
        functools.partial(kernel, n, qbits, dbits),
        out_shape=(
            jax.ShapeDtypeStruct((1, 1), F32),
            jax.ShapeDtypeStruct((c, width), F32),
            jax.ShapeDtypeStruct((c, width), F32),
        ),
        in_specs=[vmem] * 3,
        out_specs=(vmem, vmem, vmem),
        scratch_shapes=[
            pltpu.VMEM((nq * c, width), BF16),
            pltpu.VMEM((nd * c, width), BF16),
            pltpu.VMEM((1, nq * c), jnp.int32),
            pltpu.VMEM((nd * c, nq * c), F32),
            pltpu.VMEM((nd * c, nq * c), BF16),
            pltpu.VMEM((nq, 2, nq * c), F32),
            pltpu.VMEM((nd, 1, c), F32),
            pltpu.VMEM((nq * c, width), F32),
            pltpu.VMEM((nd * c, width), F32),
            pltpu.VMEM((nq * c, width), F32),
            pltpu.VMEM((nd * c, width), F32),
            dma((nq, PIECES)), dma((nq, PIECES)), dma((nd, PIECES)), dma((nd, PIECES)),
            dma((nq,)), dma((nq,)), dma((nq,)), dma((nq,)), dma((nd,)), dma((nd,)),
            dma((nq, PIECES)), dma((nq, PIECES)), dma((nd, PIECES)), dma((nd, PIECES)),
        ],
        compiler_params=pltpu.CompilerParams(
            collective_id=0, has_side_effects=True, vmem_limit_bytes=56 * 1024 * 1024
        ),
        cost_estimate=pl.CostEstimate(
            flops=6 * nq * c * nd * c * width,
            bytes_accessed=12 * c * width,
            transcendentals=nq * c * nd * c,
        ),
    )(queries, documents, positives.reshape(1, c))
    return (loss.reshape(()), grad_q, grad_d)


def solution(mesh):
    placed = (P("dp", None), P("dp", None), P("dp"))
    return jax.shard_map(
        local,
        mesh=mesh,
        in_specs=placed,
        out_specs=(P(), P("dp", None), P("dp", None)),
        check_vma=False,
    )
```

```python
import functools
import math

import jax
import jax.numpy as jnp
from jax import lax
from jax.experimental import pallas as pl
from jax.experimental.pallas import tpu as pltpu
from jax.sharding import PartitionSpec as P

PIECES = 2
F32 = jnp.float32
BF16 = jnp.bfloat16


def tree_sum(terms):
    while len(terms) > 1:
        terms = [terms[i] + terms[i + 1] for i in range(0, len(terms), 2)]
    return terms[0]


def normalize(values):
    wide = values.astype(F32)
    length = jnp.sqrt(jnp.sum(wide * wide, axis=1, keepdims=True) + 1e-06)
    return wide / length, length


def project(grad, unit, length):
    return (grad - jnp.sum(grad * unit, axis=1, keepdims=True) * unit) / length


def group_bits(n):
    bits = n.bit_length() - 1
    odd = [b for b in range(bits - 1, 0, -1) if b % 2 == 1]
    even = [b for b in range(bits - 1, 0, -1) if b % 2 == 0]
    return odd + [0], even


def stage_of(slot):
    return slot.bit_length() - 1


def place_of(slot, bits):
    return sum(((slot >> j) & 1) << (len(bits) - 1 - j) for j in range(len(bits)))


def falling(high, low):
    return list(range(high - 1, low - 1, -1))


def kernel(
    n, qbits, dbits,
    q_ref, d_ref, pos_ref,
    loss_ref, sumq_ref, sumd_ref,
    qall, dall, posrow, expd, wts, stats, losses, accq, accd, wideq,
    codeq, gotq, coded, gotd, scaleq, gotsq, scaled, gotsd,
    qs_sem, qr_sem, ds_sem, dr_sem, ps_sem, pr_sem, ss_sem, sr_sem, ls_sem, lr_sem,
    aqs_sem, aqr_sem, ads_sem, adr_sem, cqs_sem, cqr_sem, cds_sem, cdr_sem,
):
    me = lax.axis_index("dp")
    c, width = q_ref.shape
    piece = c // PIECES
    nq, nd = 1 << len(qbits), 1 << len(dbits)
    half = nq // 2

    def flipped(bits, slot):
        where = me
        for j, b in enumerate(bits):
            if (slot >> j) & 1:
                where = where + (1 - 2 * (lax.rem(lax.div(me, 1 << b), 2))) * (1 << b)
        return where

    def place_q(slot):
        return place_of(slot, qbits)

    def place_d(slot):
        return place_of(slot, dbits)

    peer_q = [flipped(qbits, k) for k in range(nq)]
    peer_d = [flipped(dbits, k) for k in range(nd)]

    barrier = pltpu.get_barrier_semaphore()
    for peer in peer_q[1:] + peer_d[1:]:
        pl.semaphore_signal(barrier, inc=1, device_id=(peer,), device_id_type=pl.DeviceIdType.MESH)

    qall[pl.ds(0, c), :] = normalize(q_ref[...])[0].astype(BF16)
    dall[pl.ds(0, c), :] = normalize(d_ref[...])[0].astype(BF16)
    posrow[:, pl.ds(0, c)] = pos_ref[...]

    pl.semaphore_wait(barrier, nq + nd - 2)

    def remote(src, dst, send, recv, peer):
        return pltpu.make_async_remote_copy(
            src_ref=src, dst_ref=dst, send_sem=send, recv_sem=recv,
            device_id=(peer,), device_id_type=pl.DeviceIdType.MESH,
        )

    def gather_copy(buf, place, send, recv, peers, slot, p):
        low = slot - (1 << stage_of(slot))
        return remote(
            buf.at[pl.ds(place(low) * c + p * piece, piece), :],
            buf.at[pl.ds(place(slot) * c + p * piece, piece), :],
            send.at[slot, p], recv.at[slot, p], peers[1 << stage_of(slot)],
        )

    gq = functools.partial(gather_copy, qall, place_q, qs_sem, qr_sem, peer_q)
    gd = functools.partial(gather_copy, dall, place_d, ds_sem, dr_sem, peer_d)
    pos_copies = [
        remote(posrow.at[:, pl.ds(0, c)], posrow.at[:, pl.ds(place_q(k) * c, c)],
               ps_sem.at[k], pr_sem.at[k], peer_q[k])
        for k in range(1, nq)
    ]

    for make, bits in ((gq, qbits), (gd, dbits)):
        for p in range(PIECES):
            for j in range(len(bits)):
                make(1 << j, p).start()
    for copy in pos_copies:
        copy.start()

    def arrive(make, bits, slots):
        for slot in slots:
            for p in range(PIECES):
                make(slot, p).wait_recv()
                for j in range(stage_of(slot) + 1, len(bits)):
                    make(slot + (1 << j), p).start()

    pair = 2 * c
    bases = [peer_d[place_d(i)] * c for i in range(nd)]

    def hits(j, i):
        start = j * pair if isinstance(j, int) else pl.multiple_of(j * pair, pair)
        return lax.broadcasted_iota(jnp.int32, (c, pair), 0) == posrow[:, pl.ds(start, pair)] - bases[i]

    def score(pairs, upper):
        first = nd // 2 if upper else 0

        def step(j, carry):
            lanes = pl.ds(pl.multiple_of(j * pair, pair), pair)
            if upper:
                total, picked = stats[0, 0:1, lanes], stats[0, 1:2, lanes]
            else:
                total, picked = jnp.zeros((1, pair), F32), jnp.zeros((1, pair), F32)
            dots = lax.dot_general(
                dall[pl.ds(first * c, nd // 2 * c), :], qall[lanes, :],
                (((1,), (1,)), ((), ())), preferred_element_type=F32,
            )
            for i in range(nd // 2):
                scores = 20.0 * dots[i * c:(i + 1) * c, :]
                powers = jnp.exp(scores - 20.0)
                expd[pl.ds((first + i) * c, c), lanes] = powers
                total = total + jnp.sum(powers, axis=0, keepdims=True)
                picked = picked + jnp.sum(
                    jnp.where(hits(j, first + i), scores, 0.0), axis=0, keepdims=True
                )
            stats[0, 0:1, lanes] = total
            stats[0, 1:2, lanes] = picked
            return carry

        lax.fori_loop(pairs[0], pairs[1], step, 0)

    arrive(gq, qbits, [1])
    arrive(gq, qbits, range(2, nq, 2))
    arrive(gd, dbits, range(2, nd, 2))
    for copy in pos_copies:
        copy.wait_recv()
    score((0, nq // 4), False)
    arrive(gd, dbits, [1])
    arrive(gq, qbits, [3])
    arrive(gq, qbits, range(5, nq, 4))
    score((nq // 4, 3 * nq // 8), False)
    arrive(gd, dbits, range(3, nd, 2))
    score((0, 3 * nq // 8), True)
    arrive(gq, qbits, range(7, nq, 4))
    score((3 * nq // 8, nq // 2), False)
    score((3 * nq // 8, nq // 2), True)

    stat_copies = [
        remote(stats.at[0], stats.at[k], ss_sem.at[k], sr_sem.at[k], peer_q[k])
        for k in range(1, nq)
    ]
    for copy in stat_copies:
        copy.start()
    for copy in stat_copies:
        copy.wait_recv()

    def slot_total(row, r):
        return tree_sum(
            [stats[k, row:row + 1, pl.ds(place_q(r ^ k) * c, c)] for k in range(nq)]
        )

    totals = [slot_total(0, r) for r in range(nq)]
    losses[0] = tree_sum([20.0 + jnp.log(totals[r]) - slot_total(1, r) for r in range(nq)])
    loss_copies = [
        remote(losses.at[0], losses.at[k], ls_sem.at[k], lr_sem.at[k], peer_d[k])
        for k in range(1, nd)
    ]

    for j in range(nq // 2):
        inverse = 1.0 / jnp.concatenate(
            [totals[place_q(2 * j)], totals[place_q(2 * j + 1)]], axis=1
        )
        lanes = pl.ds(j * pair, pair)
        for i in range(nd):
            rows = pl.ds(i * c, c)
            hit = jnp.where(hits(j, i), 1.0, 0.0)
            wts[rows, lanes] = (expd[rows, lanes] * inverse - hit).astype(BF16)

    diagonal = lax.broadcasted_iota(jnp.int32, (piece, 128), 0) == lax.broadcasted_iota(
        jnp.int32, (piece, 128), 1
    )

    def narrow_copies(code, got, scale, gots, sems, peers, slot, p):
        rows = pl.ds(slot * c + p * piece, piece)
        line = slot * PIECES + p
        peer = peers[1 << stage_of(slot)]
        return (
            remote(code.at[rows, :], got.at[rows, :], sems[0].at[slot, p], sems[1].at[slot, p], peer),
            remote(scale.at[line], gots.at[line], sems[2].at[slot, p], sems[3].at[slot, p], peer),
        )

    nq_copies = functools.partial(
        narrow_copies, codeq, gotq, scaleq, gotsq, (aqs_sem, aqr_sem, cqs_sem, cqr_sem), peer_q
    )
    nd_copies = functools.partial(
        narrow_copies, coded, gotd, scaled, gotsd, (ads_sem, adr_sem, cds_sem, cdr_sem), peer_d
    )

    def wide_copy(slot, p):
        return remote(
            accq.at[pl.ds(place_q(slot) * c + p * piece, piece), :],
            wideq.at[pl.ds((slot - half) * c + p * piece, piece), :],
            aqs_sem.at[slot, p], aqr_sem.at[slot, p], peer_q[half],
        )

    def send(which, slot, p):
        if which == "q" and slot >= half:
            wide_copy(slot, p).start()
            return
        acc, place, code, scale, copies = (
            (accq, place_q, codeq, scaleq, nq_copies) if which == "q"
            else (accd, place_d, coded, scaled, nd_copies)
        )
        value = acc[pl.ds(place(slot) * c + p * piece, piece), :]
        top = jnp.maximum(jnp.max(jnp.abs(value), axis=1, keepdims=True), 1e-30)
        codes = jnp.round(value * (32767.0 / top))
        code[pl.ds(slot * c + p * piece, piece), :] = codes.astype(jnp.int32).astype(jnp.int16)
        scale[slot * PIECES + p] = jnp.sum(
            jnp.where(diagonal, top * (1.0 / 32767.0), 0.0), axis=0, keepdims=True
        )
        for copy in copies(slot, p):
            copy.start()

    def absorb(which, slots):
        for slot in slots:
            into = slot - (1 << stage_of(slot))
            for p in range(PIECES):
                if which == "q" and slot >= half:
                    wide_copy(slot, p).wait_recv()
                    value = wideq[pl.ds((slot - half) * c + p * piece, piece), :]
                else:
                    got, gots, copies = (
                        (gotq, gotsq, nq_copies) if which == "q" else (gotd, gotsd, nd_copies)
                    )
                    for copy in copies(slot, p):
                        copy.wait_recv()
                    scales = jnp.sum(
                        jnp.where(diagonal, gots[slot * PIECES + p], 0.0), axis=1, keepdims=True
                    )
                    codes = got[pl.ds(slot * c + p * piece, piece), :]
                    value = codes.astype(jnp.int32).astype(F32) * scales
                acc, place = (accq, place_q) if which == "q" else (accd, place_d)
                rows = pl.ds(place(into) * c + p * piece, piece)
                acc[rows, :] = acc[rows, :] + value
                if into and stage_of(slot) == stage_of(into) + 1:
                    send(which, into, p)

    def grad_q(slots):
        for slot in slots:
            rows = pl.ds(place_q(slot) * c, pair)
            accq[rows, :] = lax.dot_general(
                wts[:, rows], dall[...], (((0,), (0,)), ((), ())), preferred_element_type=F32
            )
            for p in range(PIECES):
                send("q", slot + half, p)

    def grad_d(slots):
        for slot in slots:
            rows = pl.ds(place_d(slot) * c, pair)
            accd[rows, :] = jnp.dot(wts[rows, :], qall[...], preferred_element_type=F32)
            for p in range(PIECES):
                send("d", slot + nd // 2, p)

    early_q, late_q = falling(half, half // 2), falling(half // 2, 0)
    grad_q(early_q[:1])
    grad_d(falling(nd // 2, nd // 4))
    grad_q(early_q[1:])
    absorb("q", [early_q[0] + half])
    grad_d(falling(nd // 4, 0))
    absorb("q", [slot + half for slot in early_q[1:]])
    grad_q(late_q)
    for copy in loss_copies:
        copy.start()

    absorb("d", falling(nd, 3 * nd // 4))
    absorb("q", [slot + half for slot in late_q])
    rest_q, rest_d = falling(half, 1), falling(3 * nd // 4, 1)
    for i in range(max(len(rest_q), len(rest_d))):
        absorb("q", rest_q[i:i + 1])
        absorb("d", rest_d[i:i + 1])

    sumq_ref[...] = 20.0 * accq[pl.ds(0, c), :]
    sumd_ref[...] = 20.0 * accd[pl.ds(0, c), :]

    for copy in loss_copies:
        copy.wait_recv()
    row = tree_sum([losses[k] for k in range(nd)])
    loss_ref[...] = jnp.sum(row, axis=1, keepdims=True) / (c * n)

    for p in range(PIECES):
        for slot in range(1, nq):
            gq(slot, p).wait_send()
            for copy in nq_copies(slot, p) if slot < half else (wide_copy(slot, p),):
                copy.wait_send()
        for slot in range(1, nd):
            gd(slot, p).wait_send()
            for copy in nd_copies(slot, p):
                copy.wait_send()
    for copy in pos_copies + stat_copies + loss_copies:
        copy.wait_send()


def finish(q_ref, d_ref, sumq_ref, sumd_ref, outq_ref, outd_ref):
    outq_ref[...] = project(sumq_ref[...], *normalize(q_ref[...]))
    outd_ref[...] = project(sumd_ref[...], *normalize(d_ref[...]))


def local(queries, documents, positives):
    n = lax.axis_size("dp")
    c, width = queries.shape
    qbits, dbits = group_bits(n)
    nq, nd = 1 << len(qbits), 1 << len(dbits)
    dma = pltpu.SemaphoreType.DMA
    vmem = pl.BlockSpec(memory_space=pltpu.VMEM)
    tile = jax.ShapeDtypeStruct((c, width), F32)
    buffers = [
        ((nq * c, width), BF16),
        ((nd * c, width), BF16),
        ((1, nq * c), jnp.int32),
        ((nd * c, nq * c), F32),
        ((nd * c, nq * c), BF16),
        ((nq, 2, nq * c), F32),
        ((nd, 1, c), F32),
        ((nq * c, width), F32),
        ((nd * c, width), F32),
        ((nq // 2 * c, width), F32),
        ((nq // 2 * c, width), jnp.int16),
        ((nq // 2 * c, width), jnp.int16),
        ((nd * c, width), jnp.int16),
        ((nd * c, width), jnp.int16),
        ((nq // 2 * PIECES, 1, 128), F32),
        ((nq // 2 * PIECES, 1, 128), F32),
        ((nd * PIECES, 1, 128), F32),
        ((nd * PIECES, 1, 128), F32),
    ]
    held = sum(math.prod(shape) * jnp.dtype(kind).itemsize for shape, kind in buffers)
    loss, sum_q, sum_d = pl.pallas_call(
        functools.partial(kernel, n, qbits, dbits),
        out_shape=(jax.ShapeDtypeStruct((1, 1), F32), tile, tile),
        in_specs=[vmem] * 3,
        out_specs=(vmem, vmem, vmem),
        scratch_shapes=[pltpu.VMEM(shape, kind) for shape, kind in buffers] + [
            dma((nq, PIECES)), dma((nq, PIECES)), dma((nd, PIECES)), dma((nd, PIECES)),
            dma((nq,)), dma((nq,)), dma((nq,)), dma((nq,)), dma((nd,)), dma((nd,)),
            dma((nq, PIECES)), dma((nq, PIECES)), dma((nd, PIECES)), dma((nd, PIECES)),
            dma((nq, PIECES)), dma((nq, PIECES)), dma((nd, PIECES)), dma((nd, PIECES)),
        ],
        compiler_params=pltpu.CompilerParams(
            collective_id=0, has_side_effects=True,
            vmem_limit_bytes=min(held + (12 << 20), 56 << 20),
        ),
        cost_estimate=pl.CostEstimate(
            flops=6 * nq * c * nd * c * width,
            bytes_accessed=12 * c * width,
            transcendentals=nq * c * nd * c,
        ),
    )(queries, documents, positives.reshape(1, c))
    grad_q, grad_d = pl.pallas_call(
        finish,
        out_shape=(tile, tile),
        in_specs=[vmem] * 4,
        out_specs=(vmem, vmem),
        cost_estimate=pl.CostEstimate(
            flops=16 * c * width, bytes_accessed=20 * c * width, transcendentals=0
        ),
    )(queries, documents, sum_q, sum_d)
    return (loss.reshape(()), grad_q, grad_d)


def solution(mesh):
    placed = (P("dp", None), P("dp", None), P("dp"))
    return jax.shard_map(
        local,
        mesh=mesh,
        in_specs=placed,
        out_specs=(P(), P("dp", None), P("dp", None)),
        check_vma=False,
    )
```

```python
import functools

import jax
import jax.numpy as jnp
from jax import lax
from jax.experimental import pallas as pl
from jax.experimental.pallas import tpu as pltpu
from jax.sharding import PartitionSpec as P

PIECES = 2
F32 = jnp.float32
BF16 = jnp.bfloat16


def tree_sum(terms):
    while len(terms) > 1:
        terms = [terms[i] + terms[i + 1] for i in range(0, len(terms), 2)]
    return terms[0]


def normalize(values):
    wide = values.astype(F32)
    length = jnp.sqrt(jnp.sum(wide * wide, axis=1, keepdims=True) + 1e-06)
    return wide / length, length


def project(grad, unit, length):
    return (grad - jnp.sum(grad * unit, axis=1, keepdims=True) * unit) / length


def group_bits(n):
    bits = n.bit_length() - 1
    odd = [b for b in range(bits - 1, 0, -1) if b % 2 == 1]
    even = [b for b in range(bits - 1, 0, -1) if b % 2 == 0]
    return odd + [0], even


def stage_of(slot):
    return slot.bit_length() - 1


def place_of(slot, bits):
    return sum(((slot >> j) & 1) << (len(bits) - 1 - j) for j in range(len(bits)))


def falling(high, low):
    return list(range(high - 1, low - 1, -1))


def kernel(
    n, qbits, dbits,
    q_ref, d_ref, pos_ref,
    loss_ref, outq_ref, outd_ref,
    qown, down, qall, dall, posrow, expd, wts, stats, losses, accq, accd, wideq,
    codeq, gotq, coded, gotd, scaleq, gotsq, scaled, gotsd,
    qs_sem, qr_sem, ds_sem, dr_sem, ps_sem, pr_sem, ss_sem, sr_sem, ls_sem, lr_sem,
    aqs_sem, aqr_sem, ads_sem, adr_sem, cqs_sem, cqr_sem, cds_sem, cdr_sem, io_sem,
):
    me = lax.axis_index("dp")
    c, width = q_ref.shape
    piece = c // PIECES
    nq, nd = 1 << len(qbits), 1 << len(dbits)
    half = nq // 2

    def flipped(bits, slot):
        where = me
        for j, b in enumerate(bits):
            if (slot >> j) & 1:
                where = where + (1 - 2 * (lax.rem(lax.div(me, 1 << b), 2))) * (1 << b)
        return where

    def place_q(slot):
        return place_of(slot, qbits)

    def place_d(slot):
        return place_of(slot, dbits)

    peer_q = [flipped(qbits, k) for k in range(nq)]
    peer_d = [flipped(dbits, k) for k in range(nd)]

    loads = [
        pltpu.make_async_copy(q_ref, qown, io_sem.at[0]),
        pltpu.make_async_copy(d_ref, down, io_sem.at[1]),
        pltpu.make_async_copy(pos_ref, posrow.at[:, pl.ds(0, c)], io_sem.at[2]),
    ]
    for copy in loads:
        copy.start()
    barrier = pltpu.get_barrier_semaphore()
    for peer in peer_q[1:] + peer_d[1:]:
        pl.semaphore_signal(barrier, inc=1, device_id=(peer,), device_id_type=pl.DeviceIdType.MESH)

    for copy in loads:
        copy.wait()
    qall[pl.ds(0, c), :] = normalize(qown[...])[0].astype(BF16)
    dall[pl.ds(0, c), :] = normalize(down[...])[0].astype(BF16)

    pl.semaphore_wait(barrier, nq + nd - 2)

    def remote(src, dst, send, recv, peer):
        return pltpu.make_async_remote_copy(
            src_ref=src, dst_ref=dst, send_sem=send, recv_sem=recv,
            device_id=(peer,), device_id_type=pl.DeviceIdType.MESH,
        )

    def gather_copy(buf, place, send, recv, peers, slot, p):
        low = slot - (1 << stage_of(slot))
        return remote(
            buf.at[pl.ds(place(low) * c + p * piece, piece), :],
            buf.at[pl.ds(place(slot) * c + p * piece, piece), :],
            send.at[slot, p], recv.at[slot, p], peers[1 << stage_of(slot)],
        )

    gq = functools.partial(gather_copy, qall, place_q, qs_sem, qr_sem, peer_q)
    gd = functools.partial(gather_copy, dall, place_d, ds_sem, dr_sem, peer_d)
    pos_copies = [
        remote(posrow.at[:, pl.ds(0, c)], posrow.at[:, pl.ds(place_q(k) * c, c)],
               ps_sem.at[k], pr_sem.at[k], peer_q[k])
        for k in range(1, nq)
    ]

    for make, bits in ((gq, qbits), (gd, dbits)):
        for p in range(PIECES):
            for j in range(len(bits)):
                make(1 << j, p).start()
    for copy in pos_copies:
        copy.start()

    def arrive(make, bits, slots):
        for slot in slots:
            for p in range(PIECES):
                make(slot, p).wait_recv()
                for j in range(stage_of(slot) + 1, len(bits)):
                    make(slot + (1 << j), p).start()

    pair = 2 * c
    bases = [peer_d[place_d(i)] * c for i in range(nd)]

    def hits(j, i):
        start = j * pair if isinstance(j, int) else pl.multiple_of(j * pair, pair)
        return lax.broadcasted_iota(jnp.int32, (c, pair), 0) == posrow[:, pl.ds(start, pair)] - bases[i]

    def score(pairs, first, last):

        def step(j, carry):
            lanes = pl.ds(pl.multiple_of(j * pair, pair), pair)
            if first:
                total, picked = stats[0, 0:1, lanes], stats[0, 1:2, lanes]
            else:
                total, picked = jnp.zeros((1, pair), F32), jnp.zeros((1, pair), F32)
            dots = lax.dot_general(
                dall[pl.ds(first * c, (last - first) * c), :], qall[lanes, :],
                (((1,), (1,)), ((), ())), preferred_element_type=F32,
            )
            for i in range(first, last):
                scores = 20.0 * dots[(i - first) * c:(i - first + 1) * c, :]
                powers = jnp.exp(scores - 20.0)
                expd[pl.ds(i * c, c), lanes] = powers
                total = total + jnp.sum(powers, axis=0, keepdims=True)
                picked = picked + jnp.sum(
                    jnp.where(hits(j, i), scores, 0.0), axis=0, keepdims=True
                )
            stats[0, 0:1, lanes] = total
            stats[0, 1:2, lanes] = picked
            return carry

        lax.fori_loop(pairs[0], pairs[1], step, 0)

    arrive(gq, qbits, [1])
    arrive(gq, qbits, range(2, nq, 2))
    arrive(gd, dbits, range(2, nd, 2))
    for copy in pos_copies:
        copy.wait_recv()
    low, high = nd // 2, 3 * nd // 4
    score((0, nq // 4), 0, low)
    arrive(gd, dbits, [1])
    arrive(gq, qbits, [3])
    arrive(gq, qbits, range(5, nq, 4))
    arrive(gd, dbits, range(5, nd, 4))
    score((nq // 4, 3 * nq // 8), 0, low)
    score((0, 3 * nq // 8), low, high)
    arrive(gq, qbits, range(7, nq, 4))
    score((3 * nq // 8, nq // 2), 0, high)
    arrive(gd, dbits, range(3, nd, 4))
    score((0, nq // 2), high, nd)

    stat_copies = [
        remote(stats.at[0], stats.at[k], ss_sem.at[k], sr_sem.at[k], peer_q[k])
        for k in range(1, nq)
    ]
    for copy in stat_copies:
        copy.start()
    for copy in stat_copies:
        copy.wait_recv()

    def slot_total(row, r):
        return tree_sum(
            [stats[k, row:row + 1, pl.ds(place_q(r ^ k) * c, c)] for k in range(nq)]
        )

    totals = [slot_total(0, r) for r in range(nq)]
    losses[0] = tree_sum([20.0 + jnp.log(totals[r]) - slot_total(1, r) for r in range(nq)])
    loss_copies = [
        remote(losses.at[0], losses.at[k], ls_sem.at[k], lr_sem.at[k], peer_d[k])
        for k in range(1, nd)
    ]

    for j in range(nq // 2):
        inverse = 1.0 / jnp.concatenate(
            [totals[place_q(2 * j)], totals[place_q(2 * j + 1)]], axis=1
        )
        lanes = pl.ds(j * pair, pair)
        for i in range(nd):
            rows = pl.ds(i * c, c)
            hit = jnp.where(hits(j, i), 1.0, 0.0)
            wts[rows, lanes] = (expd[rows, lanes] * inverse - hit).astype(BF16)

    diagonal = lax.broadcasted_iota(jnp.int32, (piece, 128), 0) == lax.broadcasted_iota(
        jnp.int32, (piece, 128), 1
    )

    def narrow_copies(code, got, scale, gots, sems, peers, slot, p):
        rows = pl.ds(slot * c + p * piece, piece)
        line = slot * PIECES + p
        peer = peers[1 << stage_of(slot)]
        return (
            remote(code.at[rows, :], got.at[rows, :], sems[0].at[slot, p], sems[1].at[slot, p], peer),
            remote(scale.at[line], gots.at[line], sems[2].at[slot, p], sems[3].at[slot, p], peer),
        )

    nq_copies = functools.partial(
        narrow_copies, codeq, gotq, scaleq, gotsq, (aqs_sem, aqr_sem, cqs_sem, cqr_sem), peer_q
    )
    nd_copies = functools.partial(
        narrow_copies, coded, gotd, scaled, gotsd, (ads_sem, adr_sem, cds_sem, cdr_sem), peer_d
    )

    def wide_copy(slot, p):
        return remote(
            accq.at[pl.ds(place_q(slot) * c + p * piece, piece), :],
            wideq.at[pl.ds((slot - half) * c + p * piece, piece), :],
            aqs_sem.at[slot, p], aqr_sem.at[slot, p], peer_q[half],
        )

    def send(which, slot, p):
        if which == "q" and slot >= half:
            wide_copy(slot, p).start()
            return
        acc, place, code, scale, copies = (
            (accq, place_q, codeq, scaleq, nq_copies) if which == "q"
            else (accd, place_d, coded, scaled, nd_copies)
        )
        value = acc[pl.ds(place(slot) * c + p * piece, piece), :]
        top = jnp.maximum(jnp.max(jnp.abs(value), axis=1, keepdims=True), 1e-30)
        codes = jnp.round(value * (32767.0 / top))
        code[pl.ds(slot * c + p * piece, piece), :] = codes.astype(jnp.int32).astype(jnp.int16)
        scale[slot * PIECES + p] = jnp.sum(
            jnp.where(diagonal, top * (1.0 / 32767.0), 0.0), axis=0, keepdims=True
        )
        for copy in copies(slot, p):
            copy.start()

    def absorb(which, slots):
        for slot in slots:
            into = slot - (1 << stage_of(slot))
            for p in range(PIECES):
                if which == "q" and slot >= half:
                    wide_copy(slot, p).wait_recv()
                    value = wideq[pl.ds((slot - half) * c + p * piece, piece), :]
                else:
                    got, gots, copies = (
                        (gotq, gotsq, nq_copies) if which == "q" else (gotd, gotsd, nd_copies)
                    )
                    for copy in copies(slot, p):
                        copy.wait_recv()
                    scales = jnp.sum(
                        jnp.where(diagonal, gots[slot * PIECES + p], 0.0), axis=1, keepdims=True
                    )
                    codes = got[pl.ds(slot * c + p * piece, piece), :]
                    value = codes.astype(jnp.int32).astype(F32) * scales
                acc, place = (accq, place_q) if which == "q" else (accd, place_d)
                rows = pl.ds(place(into) * c + p * piece, piece)
                acc[rows, :] = acc[rows, :] + value
                if into and stage_of(slot) == stage_of(into) + 1:
                    send(which, into, p)

    def grad_q(slots):
        for slot in slots:
            rows = pl.ds(place_q(slot) * c, pair)
            accq[rows, :] = lax.dot_general(
                wts[:, rows], dall[...], (((0,), (0,)), ((), ())), preferred_element_type=F32
            )
            for p in range(PIECES):
                send("q", slot + half, p)

    def grad_d(slots):
        for slot in slots:
            rows = pl.ds(place_d(slot) * c, pair)
            accd[rows, :] = jnp.dot(wts[rows, :], qall[...], preferred_element_type=F32)
            for p in range(PIECES):
                send("d", slot + nd // 2, p)

    early_q, late_q = falling(half, half // 2), falling(half // 2, 0)
    grad_d(falling(nd // 2, nd // 4))
    grad_q(early_q)
    absorb("q", [early_q[0] + half])
    grad_d(falling(nd // 4, 0))
    absorb("q", [slot + half for slot in early_q[1:]])
    grad_q(late_q)
    for copy in loss_copies:
        copy.start()

    absorb("d", falling(nd, 3 * nd // 4))
    absorb("q", [slot + half for slot in late_q])
    rest_q, rest_d = falling(half, 1), falling(3 * nd // 4, 1)
    for i in range(max(len(rest_q), len(rest_d))):
        absorb("q", rest_q[i:i + 1])
        absorb("d", rest_d[i:i + 1])

    own = pl.ds(0, c)
    stores = [
        pltpu.make_async_copy(accq.at[own, :], outq_ref, io_sem.at[3]),
        pltpu.make_async_copy(accd.at[own, :], outd_ref, io_sem.at[4]),
    ]
    accq[own, :] = project(20.0 * accq[own, :], *normalize(qown[...]))
    stores[0].start()
    accd[own, :] = project(20.0 * accd[own, :], *normalize(down[...]))
    stores[1].start()

    for copy in loss_copies:
        copy.wait_recv()
    row = tree_sum([losses[k] for k in range(nd)])
    loss_ref[...] = jnp.sum(row, axis=1, keepdims=True) / (c * n)

    for p in range(PIECES):
        for slot in range(1, nq):
            gq(slot, p).wait_send()
            for copy in nq_copies(slot, p) if slot < half else (wide_copy(slot, p),):
                copy.wait_send()
        for slot in range(1, nd):
            gd(slot, p).wait_send()
            for copy in nd_copies(slot, p):
                copy.wait_send()
    for copy in pos_copies + stat_copies + loss_copies:
        copy.wait_send()
    for copy in stores:
        copy.wait()


def local(queries, documents, positives):
    n = lax.axis_size("dp")
    c, width = queries.shape
    qbits, dbits = group_bits(n)
    nq, nd = 1 << len(qbits), 1 << len(dbits)
    dma = pltpu.SemaphoreType.DMA
    vmem = pl.BlockSpec(memory_space=pltpu.VMEM)
    tile = jax.ShapeDtypeStruct((c, width), F32)
    anywhere = pl.BlockSpec(memory_space=pl.ANY)
    buffers = [
        ((c, width), BF16),
        ((c, width), BF16),
        ((nq * c, width), BF16),
        ((nd * c, width), BF16),
        ((1, nq * c), jnp.int32),
        ((nd * c, nq * c), F32),
        ((nd * c, nq * c), BF16),
        ((nq, 2, nq * c), F32),
        ((nd, 1, c), F32),
        ((nq * c, width), F32),
        ((nd * c, width), F32),
        ((nq // 2 * c, width), F32),
        ((nq // 2 * c, width), jnp.int16),
        ((nq // 2 * c, width), jnp.int16),
        ((nd * c, width), jnp.int16),
        ((nd * c, width), jnp.int16),
        ((nq // 2 * PIECES, 1, 128), F32),
        ((nq // 2 * PIECES, 1, 128), F32),
        ((nd * PIECES, 1, 128), F32),
        ((nd * PIECES, 1, 128), F32),
    ]
    loss, grad_q, grad_d = pl.pallas_call(
        functools.partial(kernel, n, qbits, dbits),
        out_shape=(jax.ShapeDtypeStruct((1, 1), F32), tile, tile),
        in_specs=[anywhere] * 3,
        out_specs=(vmem, anywhere, anywhere),
        scratch_shapes=[pltpu.VMEM(shape, kind) for shape, kind in buffers] + [
            dma((nq, PIECES)), dma((nq, PIECES)), dma((nd, PIECES)), dma((nd, PIECES)),
            dma((nq,)), dma((nq,)), dma((nq,)), dma((nq,)), dma((nd,)), dma((nd,)),
            dma((nq, PIECES)), dma((nq, PIECES)), dma((nd, PIECES)), dma((nd, PIECES)),
            dma((nq, PIECES)), dma((nq, PIECES)), dma((nd, PIECES)), dma((nd, PIECES)),
            dma((5,)),
        ],
        compiler_params=pltpu.CompilerParams(
            collective_id=0, has_side_effects=True,
            vmem_limit_bytes=56 << 20,
        ),
        cost_estimate=pl.CostEstimate(
            flops=6 * nq * c * nd * c * width,
            bytes_accessed=12 * c * width,
            transcendentals=nq * c * nd * c,
        ),
    )(queries, documents, positives.reshape(1, c))
    return (loss.reshape(()), grad_q, grad_d)


def solution(mesh):
    placed = (P("dp", None), P("dp", None), P("dp"))
    return jax.shard_map(
        local,
        mesh=mesh,
        in_specs=placed,
        out_specs=(P(), P("dp", None), P("dp", None)),
        check_vma=False,
    )
```

```python
import functools

import jax
import jax.numpy as jnp
from jax import lax
from jax.experimental import pallas as pl
from jax.experimental.pallas import tpu as pltpu
from jax.sharding import PartitionSpec as P

PIECES = 2
VMEM_BYTES = 56 << 20
F32 = jnp.float32
BF16 = jnp.bfloat16


def tree_sum(terms):
    while len(terms) > 1:
        terms = [terms[i] + terms[i + 1] for i in range(0, len(terms), 2)]
    return terms[0]


def normalize(values):
    wide = values.astype(F32)
    length = jnp.sqrt(jnp.sum(wide * wide, axis=1, keepdims=True) + 1e-06)
    return wide / length, length


def project(grad, unit, length):
    return (grad - jnp.sum(grad * unit, axis=1, keepdims=True) * unit) / length


def group_bits(n):
    bits = n.bit_length() - 1
    odd = [b for b in range(bits - 1, 0, -1) if b % 2 == 1]
    even = [b for b in range(bits - 1, 0, -1) if b % 2 == 0]
    return odd + [0], even


def stage_of(slot):
    return slot.bit_length() - 1


def place_of(slot, bits):
    return sum(((slot >> j) & 1) << (len(bits) - 1 - j) for j in range(len(bits)))


def falling(high, low):
    return list(range(high - 1, low - 1, -1))


def kernel(
    n, qbits, dbits,
    q_ref, d_ref, pos_ref,
    loss_ref, outq_ref, outd_ref,
    qown, down, qall, dall, posrow, expd, wts, stats, losses, accq, accd, wideq,
    codeq, gotq, coded, gotd, scaleq, gotsq, scaled, gotsd,
    qs_sem, qr_sem, ds_sem, dr_sem, ps_sem, pr_sem, ss_sem, sr_sem, ls_sem, lr_sem,
    aqs_sem, aqr_sem, ads_sem, adr_sem, cqs_sem, cqr_sem, cds_sem, cdr_sem, io_sem,
):
    me = lax.axis_index("dp")
    c, width = q_ref.shape
    piece = c // PIECES
    nq, nd = 1 << len(qbits), 1 << len(dbits)
    half = nq // 2

    def flipped(bits, slot):
        where = me
        for j, b in enumerate(bits):
            if (slot >> j) & 1:
                where = where + (1 - 2 * (lax.rem(lax.div(me, 1 << b), 2))) * (1 << b)
        return where

    def place_q(slot):
        return place_of(slot, qbits)

    def place_d(slot):
        return place_of(slot, dbits)

    peer_q = [flipped(qbits, k) for k in range(nq)]
    peer_d = [flipped(dbits, k) for k in range(nd)]

    loads = [
        pltpu.make_async_copy(q_ref, qown, io_sem.at[0]),
        pltpu.make_async_copy(d_ref, down, io_sem.at[1]),
        pltpu.make_async_copy(pos_ref, posrow.at[:, pl.ds(0, c)], io_sem.at[2]),
    ]
    for copy in loads:
        copy.start()
    barrier = pltpu.get_barrier_semaphore()
    for peer in peer_q[1:] + peer_d[1:]:
        pl.semaphore_signal(barrier, inc=1, device_id=(peer,), device_id_type=pl.DeviceIdType.MESH)

    for copy in loads:
        copy.wait()
    qall[pl.ds(0, c), :] = normalize(qown[...])[0].astype(BF16)
    dall[pl.ds(0, c), :] = normalize(down[...])[0].astype(BF16)

    pl.semaphore_wait(barrier, nq + nd - 2)

    def remote(src, dst, send, recv, peer):
        return pltpu.make_async_remote_copy(
            src_ref=src, dst_ref=dst, send_sem=send, recv_sem=recv,
            device_id=(peer,), device_id_type=pl.DeviceIdType.MESH,
        )

    def gather_copy(buf, place, send, recv, peers, slot, p):
        low = slot - (1 << stage_of(slot))
        return remote(
            buf.at[pl.ds(place(low) * c + p * piece, piece), :],
            buf.at[pl.ds(place(slot) * c + p * piece, piece), :],
            send.at[slot, p], recv.at[slot, p], peers[1 << stage_of(slot)],
        )

    gq = functools.partial(gather_copy, qall, place_q, qs_sem, qr_sem, peer_q)
    gd = functools.partial(gather_copy, dall, place_d, ds_sem, dr_sem, peer_d)
    pos_copies = [
        remote(posrow.at[:, pl.ds(0, c)], posrow.at[:, pl.ds(place_q(k) * c, c)],
               ps_sem.at[k], pr_sem.at[k], peer_q[k])
        for k in range(1, nq)
    ]

    for p in range(PIECES):
        for j in range(len(qbits)):
            gq(1 << j, p).start()
            if j < len(dbits):
                gd(1 << j, p).start()
    for copy in pos_copies:
        copy.start()

    def arrive(make, bits, slots):
        for slot in slots:
            for p in range(PIECES):
                make(slot, p).wait_recv()
                for j in range(stage_of(slot) + 1, len(bits)):
                    make(slot + (1 << j), p).start()

    pair = 2 * c
    bases = [peer_d[place_d(i)] * c for i in range(nd)]

    def hits(j, i):
        start = j * pair if isinstance(j, int) else pl.multiple_of(j * pair, pair)
        return lax.broadcasted_iota(jnp.int32, (c, pair), 0) == posrow[:, pl.ds(start, pair)] - bases[i]

    def score(pairs, first, last):

        def step(j, carry):
            lanes = pl.ds(pl.multiple_of(j * pair, pair), pair)
            if first:
                total, picked = stats[0, 0:1, lanes], stats[0, 1:2, lanes]
            else:
                total, picked = jnp.zeros((1, pair), F32), jnp.zeros((1, pair), F32)
            dots = lax.dot_general(
                dall[pl.ds(first * c, (last - first) * c), :], qall[lanes, :],
                (((1,), (1,)), ((), ())), preferred_element_type=F32,
            )
            for i in range(first, last):
                scores = 20.0 * dots[(i - first) * c:(i - first + 1) * c, :]
                powers = jnp.exp(scores - 20.0)
                expd[pl.ds(i * c, c), lanes] = powers
                total = total + jnp.sum(powers, axis=0, keepdims=True)
                picked = picked + jnp.sum(
                    jnp.where(hits(j, i), scores, 0.0), axis=0, keepdims=True
                )
            stats[0, 0:1, lanes] = total
            stats[0, 1:2, lanes] = picked
            return carry

        lax.fori_loop(pairs[0], pairs[1], step, 0, unroll=True)

    arrive(gq, qbits, [1])
    arrive(gq, qbits, range(2, nq, 2))
    arrive(gd, dbits, range(2, nd, 2))
    for copy in pos_copies:
        copy.wait_recv()
    low, high = nd // 2, 3 * nd // 4
    score((0, nq // 4), 0, low)
    arrive(gd, dbits, [1])
    arrive(gq, qbits, [3])
    arrive(gq, qbits, range(5, nq, 4))
    arrive(gd, dbits, range(5, nd, 4))
    score((nq // 4, 3 * nq // 8), 0, low)
    score((0, 3 * nq // 8), low, high)
    arrive(gq, qbits, range(7, nq, 4))
    score((3 * nq // 8, nq // 2), 0, high)
    arrive(gd, dbits, range(3, nd, 4))
    score((0, nq // 2), high, nd)

    stat_copies = [
        remote(stats.at[0], stats.at[k], ss_sem.at[k], sr_sem.at[k], peer_q[k])
        for k in range(1, nq)
    ]
    for copy in stat_copies:
        copy.start()
    for copy in stat_copies:
        copy.wait_recv()

    def slot_total(row, r):
        return tree_sum(
            [stats[k, row:row + 1, pl.ds(place_q(r ^ k) * c, c)] for k in range(nq)]
        )

    totals = [slot_total(0, r) for r in range(nq)]
    losses[0] = tree_sum([20.0 + jnp.log(totals[r]) - slot_total(1, r) for r in range(nq)])
    loss_copies = [
        remote(losses.at[0], losses.at[k], ls_sem.at[k], lr_sem.at[k], peer_d[k])
        for k in range(1, nd)
    ]

    inverses = [
        1.0 / jnp.concatenate([totals[place_q(2 * j)], totals[place_q(2 * j + 1)]], axis=1)
        for j in range(nq // 2)
    ]

    def weigh(places):
        for i in places:
            rows = pl.ds(i * c, c)
            for j in range(nq // 2):
                lanes = pl.ds(j * pair, pair)
                hit = jnp.where(hits(j, i), 1.0, 0.0)
                wts[rows, lanes] = (expd[rows, lanes] * inverses[j] - hit).astype(BF16)

    diagonal = lax.broadcasted_iota(jnp.int32, (piece, 128), 0) == lax.broadcasted_iota(
        jnp.int32, (piece, 128), 1
    )

    def narrow_copies(code, got, scale, gots, sems, peers, slot, p):
        rows = pl.ds(slot * c + p * piece, piece)
        line = slot * PIECES + p
        peer = peers[1 << stage_of(slot)]
        return (
            remote(code.at[rows, :], got.at[rows, :], sems[0].at[slot, p], sems[1].at[slot, p], peer),
            remote(scale.at[line], gots.at[line], sems[2].at[slot, p], sems[3].at[slot, p], peer),
        )

    nq_copies = functools.partial(
        narrow_copies, codeq, gotq, scaleq, gotsq, (aqs_sem, aqr_sem, cqs_sem, cqr_sem), peer_q
    )
    nd_copies = functools.partial(
        narrow_copies, coded, gotd, scaled, gotsd, (ads_sem, adr_sem, cds_sem, cdr_sem), peer_d
    )

    def wide_copy(slot, p):
        return remote(
            accq.at[pl.ds(place_q(slot) * c + p * piece, piece), :],
            wideq.at[pl.ds((slot - half) * c + p * piece, piece), :],
            aqs_sem.at[slot, p], aqr_sem.at[slot, p], peer_q[half],
        )

    def send(which, slot, p):
        if which == "q" and slot >= half:
            wide_copy(slot, p).start()
            return
        acc, place, code, scale, copies = (
            (accq, place_q, codeq, scaleq, nq_copies) if which == "q"
            else (accd, place_d, coded, scaled, nd_copies)
        )
        value = acc[pl.ds(place(slot) * c + p * piece, piece), :]
        top = jnp.maximum(jnp.max(jnp.abs(value), axis=1, keepdims=True), 1e-30)
        codes = jnp.round(value * (32767.0 / top))
        code[pl.ds(slot * c + p * piece, piece), :] = codes.astype(jnp.int32).astype(jnp.int16)
        scale[slot * PIECES + p] = jnp.sum(
            jnp.where(diagonal, top * (1.0 / 32767.0), 0.0), axis=0, keepdims=True
        )
        for copy in copies(slot, p):
            copy.start()

    def absorb(which, slots):
        for slot in slots:
            into = slot - (1 << stage_of(slot))
            for p in range(PIECES):
                if which == "q" and slot >= half:
                    wide_copy(slot, p).wait_recv()
                    value = wideq[pl.ds((slot - half) * c + p * piece, piece), :]
                else:
                    got, gots, copies = (
                        (gotq, gotsq, nq_copies) if which == "q" else (gotd, gotsd, nd_copies)
                    )
                    for copy in copies(slot, p):
                        copy.wait_recv()
                    scales = jnp.sum(
                        jnp.where(diagonal, gots[slot * PIECES + p], 0.0), axis=1, keepdims=True
                    )
                    codes = got[pl.ds(slot * c + p * piece, piece), :]
                    value = codes.astype(jnp.int32).astype(F32) * scales
                acc, place = (accq, place_q) if which == "q" else (accd, place_d)
                rows = pl.ds(place(into) * c + p * piece, piece)
                acc[rows, :] = acc[rows, :] + value
                if into and stage_of(slot) == stage_of(into) + 1:
                    send(which, into, p)

    def grad_q(slots):
        for slot in slots:
            rows = pl.ds(place_q(slot) * c, pair)
            accq[rows, :] = lax.dot_general(
                wts[:, rows], dall[...], (((0,), (0,)), ((), ())), preferred_element_type=F32
            )
            for p in range(PIECES):
                send("q", slot + half, p)

    def grad_d(slots):
        for slot in slots:
            rows = pl.ds(place_d(slot) * c, pair)
            accd[rows, :] = jnp.dot(wts[rows, :], qall[...], preferred_element_type=F32)
            for p in range(PIECES):
                send("d", slot + nd // 2, p)

    early_q, late_q = falling(half, half // 2), falling(half // 2, 0)
    for slot in falling(nd // 2, nd // 4):
        weigh([place_d(slot), place_d(slot) + 1])
        grad_d([slot])
    for slot in falling(nd // 4, 0):
        weigh([place_d(slot), place_d(slot) + 1])
    grad_q(early_q)
    absorb("q", [early_q[0] + half])
    grad_d(falling(nd // 4, 0))
    absorb("q", [slot + half for slot in early_q[1:]])
    grad_q(late_q)
    for copy in loss_copies:
        copy.start()

    absorb("d", falling(nd, 3 * nd // 4))
    absorb("q", [slot + half for slot in late_q])
    rest_q, rest_d = falling(half, 1), falling(3 * nd // 4, 1)
    for i in range(max(len(rest_q), len(rest_d))):
        absorb("q", rest_q[i:i + 1])
        absorb("d", rest_d[i:i + 1])

    own = pl.ds(0, c)
    stores = [
        pltpu.make_async_copy(accq.at[own, :], outq_ref, io_sem.at[3]),
        pltpu.make_async_copy(accd.at[own, :], outd_ref, io_sem.at[4]),
    ]
    accq[own, :] = project(20.0 * accq[own, :], *normalize(qown[...]))
    stores[0].start()
    accd[own, :] = project(20.0 * accd[own, :], *normalize(down[...]))
    stores[1].start()

    for copy in loss_copies:
        copy.wait_recv()
    row = tree_sum([losses[k] for k in range(nd)])
    loss_ref[...] = jnp.sum(row, axis=1, keepdims=True) / (c * n)

    for p in range(PIECES):
        for slot in range(1, nq):
            gq(slot, p).wait_send()
            for copy in nq_copies(slot, p) if slot < half else (wide_copy(slot, p),):
                copy.wait_send()
        for slot in range(1, nd):
            gd(slot, p).wait_send()
            for copy in nd_copies(slot, p):
                copy.wait_send()
    for copy in pos_copies + stat_copies + loss_copies:
        copy.wait_send()
    for copy in stores:
        copy.wait()


def hand_over(sumq_ref, sumd_ref, outq_ref, outd_ref, sem):
    copies = [
        pltpu.make_async_copy(sumq_ref, outq_ref, sem.at[0]),
        pltpu.make_async_copy(sumd_ref, outd_ref, sem.at[1]),
    ]
    for copy in copies:
        copy.start()
    for copy in copies:
        copy.wait()


def local(queries, documents, positives):
    n = lax.axis_size("dp")
    c, width = queries.shape
    qbits, dbits = group_bits(n)
    nq, nd = 1 << len(qbits), 1 << len(dbits)
    dma = pltpu.SemaphoreType.DMA
    vmem = pl.BlockSpec(memory_space=pltpu.VMEM)
    tile = jax.ShapeDtypeStruct((c, width), F32)
    anywhere = pl.BlockSpec(memory_space=pl.ANY)
    buffers = [
        ((c, width), BF16),
        ((c, width), BF16),
        ((nq * c, width), BF16),
        ((nd * c, width), BF16),
        ((1, nq * c), jnp.int32),
        ((nd * c, nq * c), F32),
        ((nd * c, nq * c), BF16),
        ((nq, 2, nq * c), F32),
        ((nd, 1, c), F32),
        ((nq * c, width), F32),
        ((nd * c, width), F32),
        ((nq // 2 * c, width), F32),
        ((nq // 2 * c, width), jnp.int16),
        ((nq // 2 * c, width), jnp.int16),
        ((nd * c, width), jnp.int16),
        ((nd * c, width), jnp.int16),
        ((nq // 2 * PIECES, 1, 128), F32),
        ((nq // 2 * PIECES, 1, 128), F32),
        ((nd * PIECES, 1, 128), F32),
        ((nd * PIECES, 1, 128), F32),
    ]
    loss, grad_q, grad_d = pl.pallas_call(
        functools.partial(kernel, n, qbits, dbits),
        out_shape=(jax.ShapeDtypeStruct((1, 1), F32), tile, tile),
        in_specs=[anywhere] * 3,
        out_specs=(vmem, anywhere, anywhere),
        scratch_shapes=[pltpu.VMEM(shape, kind) for shape, kind in buffers] + [
            dma((nq, PIECES)), dma((nq, PIECES)), dma((nd, PIECES)), dma((nd, PIECES)),
            dma((nq,)), dma((nq,)), dma((nq,)), dma((nq,)), dma((nd,)), dma((nd,)),
            dma((nq, PIECES)), dma((nq, PIECES)), dma((nd, PIECES)), dma((nd, PIECES)),
            dma((nq, PIECES)), dma((nq, PIECES)), dma((nd, PIECES)), dma((nd, PIECES)),
            dma((5,)),
        ],
        compiler_params=pltpu.CompilerParams(
            collective_id=0, has_side_effects=True,
            vmem_limit_bytes=VMEM_BYTES,
        ),
        cost_estimate=pl.CostEstimate(
            flops=6 * nq * c * nd * c * width,
            bytes_accessed=12 * c * width,
            transcendentals=nq * c * nd * c,
        ),
    )(queries, documents, positives.reshape(1, c))
    grad_q, grad_d = pl.pallas_call(
        hand_over,
        out_shape=(tile, tile),
        in_specs=[anywhere] * 2,
        out_specs=(anywhere, anywhere),
        scratch_shapes=[dma((2,))],
        compiler_params=pltpu.CompilerParams(vmem_limit_bytes=VMEM_BYTES),
        cost_estimate=pl.CostEstimate(
            flops=0, bytes_accessed=16 * c * width, transcendentals=0
        ),
    )(grad_q, grad_d)
    return (loss.reshape(()), grad_q, grad_d)


def solution(mesh):
    placed = (P("dp", None), P("dp", None), P("dp"))
    return jax.shard_map(
        local,
        mesh=mesh,
        in_specs=placed,
        out_specs=(P(), P("dp", None), P("dp", None)),
        check_vma=False,
    )
```

```python
import functools

import jax
import jax.numpy as jnp
from jax import lax
from jax.experimental import pallas as pl
from jax.experimental.pallas import tpu as pltpu
from jax.sharding import PartitionSpec as P

PIECES = 4
VMEM_BYTES = 56 << 20
F32 = jnp.float32
BF16 = jnp.bfloat16


def tree_sum(terms):
    while len(terms) > 1:
        terms = [terms[i] + terms[i + 1] for i in range(0, len(terms), 2)]
    return terms[0]


def normalize(values):
    wide = values.astype(F32)
    length = jnp.sqrt(jnp.sum(wide * wide, axis=1, keepdims=True) + 1e-06)
    return wide / length, length


def project(grad, unit, length):
    return (grad - jnp.sum(grad * unit, axis=1, keepdims=True) * unit) / length


def group_bits(n):
    bits = n.bit_length() - 1
    odd = [b for b in range(bits - 1, 0, -1) if b % 2 == 1]
    even = [b for b in range(bits - 1, 0, -1) if b % 2 == 0]
    return odd + [0], even


def stage_of(slot):
    return slot.bit_length() - 1


def place_of(slot, bits):
    return sum(((slot >> j) & 1) << (len(bits) - 1 - j) for j in range(len(bits)))


def falling(high, low):
    return list(range(high - 1, low - 1, -1))


def kernel(
    n, qbits, dbits,
    q_ref, d_ref, pos_ref,
    loss_ref, outq_ref, outd_ref,
    qown, down, qall, dall, posrow, expd, wts, stats, losses, accq, accd, wideq,
    codeq, gotq, coded, gotd, scaleq, gotsq, scaled, gotsd,
    qs_sem, qr_sem, ds_sem, dr_sem, ps_sem, pr_sem, ss_sem, sr_sem, ls_sem, lr_sem,
    aqs_sem, aqr_sem, ads_sem, adr_sem, cqs_sem, cqr_sem, cds_sem, cdr_sem, io_sem,
):
    me = lax.axis_index("dp")
    c, width = q_ref.shape
    piece = c // PIECES
    nq, nd = 1 << len(qbits), 1 << len(dbits)
    half = nq // 2

    def flipped(bits, slot):
        where = me
        for j, b in enumerate(bits):
            if (slot >> j) & 1:
                where = where + (1 - 2 * (lax.rem(lax.div(me, 1 << b), 2))) * (1 << b)
        return where

    def place_q(slot):
        return place_of(slot, qbits)

    def place_d(slot):
        return place_of(slot, dbits)

    peer_q = [flipped(qbits, k) for k in range(nq)]
    peer_d = [flipped(dbits, k) for k in range(nd)]

    loads = [
        pltpu.make_async_copy(q_ref, qown, io_sem.at[0]),
        pltpu.make_async_copy(d_ref, down, io_sem.at[1]),
        pltpu.make_async_copy(pos_ref, posrow.at[:, pl.ds(0, c)], io_sem.at[2]),
    ]
    for copy in loads:
        copy.start()
    barrier = pltpu.get_barrier_semaphore()
    for peer in peer_q[1:] + peer_d[1:]:
        pl.semaphore_signal(barrier, inc=1, device_id=(peer,), device_id_type=pl.DeviceIdType.MESH)

    for copy in loads:
        copy.wait()
    qall[pl.ds(0, c), :] = normalize(qown[...])[0].astype(BF16)
    dall[pl.ds(0, c), :] = normalize(down[...])[0].astype(BF16)

    pl.semaphore_wait(barrier, nq + nd - 2)

    def remote(src, dst, send, recv, peer):
        return pltpu.make_async_remote_copy(
            src_ref=src, dst_ref=dst, send_sem=send, recv_sem=recv,
            device_id=(peer,), device_id_type=pl.DeviceIdType.MESH,
        )

    def gather_copy(buf, place, send, recv, peers, slot, p):
        low = slot - (1 << stage_of(slot))
        return remote(
            buf.at[pl.ds(place(low) * c + p * piece, piece), :],
            buf.at[pl.ds(place(slot) * c + p * piece, piece), :],
            send.at[slot, p], recv.at[slot, p], peers[1 << stage_of(slot)],
        )

    gq = functools.partial(gather_copy, qall, place_q, qs_sem, qr_sem, peer_q)
    gd = functools.partial(gather_copy, dall, place_d, ds_sem, dr_sem, peer_d)
    pos_copies = [
        remote(posrow.at[:, pl.ds(0, c)], posrow.at[:, pl.ds(place_q(k) * c, c)],
               ps_sem.at[k], pr_sem.at[k], peer_q[k])
        for k in range(1, nq)
    ]

    for p in range(PIECES):
        for j in range(len(qbits)):
            gq(1 << j, p).start()
            if j < len(dbits):
                gd(1 << j, p).start()
    for copy in pos_copies:
        copy.start()

    def arrive(make, bits, slots):
        for slot in slots:
            for p in range(PIECES):
                make(slot, p).wait_recv()
                for j in range(stage_of(slot) + 1, len(bits)):
                    make(slot + (1 << j), p).start()

    pair = 2 * c
    bases = [peer_d[place_d(i)] * c for i in range(nd)]

    def hits(j, i):
        start = j * pair if isinstance(j, int) else pl.multiple_of(j * pair, pair)
        return lax.broadcasted_iota(jnp.int32, (c, pair), 0) == posrow[:, pl.ds(start, pair)] - bases[i]

    def score(pairs, first, last):

        def step(j, carry):
            lanes = pl.ds(pl.multiple_of(j * pair, pair), pair)
            if first:
                total, picked = stats[0, 0:1, lanes], stats[0, 1:2, lanes]
            else:
                total, picked = jnp.zeros((1, pair), F32), jnp.zeros((1, pair), F32)
            dots = lax.dot_general(
                dall[pl.ds(first * c, (last - first) * c), :], qall[lanes, :],
                (((1,), (1,)), ((), ())), preferred_element_type=F32,
            )
            for i in range(first, last):
                scores = 20.0 * dots[(i - first) * c:(i - first + 1) * c, :]
                powers = jnp.exp(scores - 20.0)
                expd[pl.ds(i * c, c), lanes] = powers
                total = total + jnp.sum(powers, axis=0, keepdims=True)
                picked = picked + jnp.sum(
                    jnp.where(hits(j, i), scores, 0.0), axis=0, keepdims=True
                )
            stats[0, 0:1, lanes] = total
            stats[0, 1:2, lanes] = picked
            return carry

        lax.fori_loop(pairs[0], pairs[1], step, 0, unroll=True)

    arrive(gq, qbits, [1])
    arrive(gq, qbits, range(2, nq, 2))
    arrive(gd, dbits, range(2, nd, 2))
    for copy in pos_copies:
        copy.wait_recv()
    low, high = nd // 2, 3 * nd // 4
    score((0, nq // 4), 0, low)
    arrive(gd, dbits, [1])
    arrive(gq, qbits, [3])
    arrive(gq, qbits, range(5, nq, 4))
    arrive(gd, dbits, range(5, nd, 4))
    score((nq // 4, 3 * nq // 8), 0, low)
    score((0, 3 * nq // 8), low, high)
    arrive(gq, qbits, range(7, nq, 4))
    score((3 * nq // 8, nq // 2), 0, high)
    arrive(gd, dbits, range(3, nd, 4))
    score((0, nq // 2), high, nd)

    stat_copies = [
        remote(stats.at[0], stats.at[k], ss_sem.at[k], sr_sem.at[k], peer_q[k])
        for k in range(1, nq)
    ]
    for copy in stat_copies:
        copy.start()
    for copy in stat_copies:
        copy.wait_recv()

    def slot_total(row, r):
        return tree_sum(
            [stats[k, row:row + 1, pl.ds(place_q(r ^ k) * c, c)] for k in range(nq)]
        )

    totals = [slot_total(0, r) for r in range(nq)]
    losses[0] = tree_sum([20.0 + jnp.log(totals[r]) - slot_total(1, r) for r in range(nq)])
    loss_copies = [
        remote(losses.at[0], losses.at[k], ls_sem.at[k], lr_sem.at[k], peer_d[k])
        for k in range(1, nd)
    ]

    inverses = [
        1.0 / jnp.concatenate([totals[place_q(2 * j)], totals[place_q(2 * j + 1)]], axis=1)
        for j in range(nq // 2)
    ]

    def weigh(places):
        for i in places:
            rows = pl.ds(i * c, c)
            for j in range(nq // 2):
                lanes = pl.ds(j * pair, pair)
                hit = jnp.where(hits(j, i), 1.0, 0.0)
                wts[rows, lanes] = (expd[rows, lanes] * inverses[j] - hit).astype(BF16)

    diagonal = lax.broadcasted_iota(jnp.int32, (piece, 128), 0) == lax.broadcasted_iota(
        jnp.int32, (piece, 128), 1
    )

    def narrow_copies(code, got, scale, gots, sems, peers, slot, p):
        rows = pl.ds(slot * c + p * piece, piece)
        line = slot * PIECES + p
        peer = peers[1 << stage_of(slot)]
        return (
            remote(code.at[rows, :], got.at[rows, :], sems[0].at[slot, p], sems[1].at[slot, p], peer),
            remote(scale.at[line], gots.at[line], sems[2].at[slot, p], sems[3].at[slot, p], peer),
        )

    nq_copies = functools.partial(
        narrow_copies, codeq, gotq, scaleq, gotsq, (aqs_sem, aqr_sem, cqs_sem, cqr_sem), peer_q
    )
    nd_copies = functools.partial(
        narrow_copies, coded, gotd, scaled, gotsd, (ads_sem, adr_sem, cds_sem, cdr_sem), peer_d
    )

    def wide_copy(slot, p):
        return remote(
            accq.at[pl.ds(place_q(slot) * c + p * piece, piece), :],
            wideq.at[pl.ds((slot - half) * c + p * piece, piece), :],
            aqs_sem.at[slot, p], aqr_sem.at[slot, p], peer_q[half],
        )

    def send(which, slot, p):
        if which == "q" and slot >= half:
            wide_copy(slot, p).start()
            return
        acc, place, code, scale, copies = (
            (accq, place_q, codeq, scaleq, nq_copies) if which == "q"
            else (accd, place_d, coded, scaled, nd_copies)
        )
        value = acc[pl.ds(place(slot) * c + p * piece, piece), :]
        top = jnp.maximum(jnp.max(jnp.abs(value), axis=1, keepdims=True), 1e-30)
        codes = jnp.round(value * (32767.0 / top))
        code[pl.ds(slot * c + p * piece, piece), :] = codes.astype(jnp.int32).astype(jnp.int16)
        scale[slot * PIECES + p] = jnp.sum(
            jnp.where(diagonal, top * (1.0 / 32767.0), 0.0), axis=0, keepdims=True
        )
        for copy in copies(slot, p):
            copy.start()

    def absorb(which, slots):
        for slot in slots:
            into = slot - (1 << stage_of(slot))
            for p in range(PIECES):
                if which == "q" and slot >= half:
                    wide_copy(slot, p).wait_recv()
                    value = wideq[pl.ds((slot - half) * c + p * piece, piece), :]
                else:
                    got, gots, copies = (
                        (gotq, gotsq, nq_copies) if which == "q" else (gotd, gotsd, nd_copies)
                    )
                    for copy in copies(slot, p):
                        copy.wait_recv()
                    scales = jnp.sum(
                        jnp.where(diagonal, gots[slot * PIECES + p], 0.0), axis=1, keepdims=True
                    )
                    codes = got[pl.ds(slot * c + p * piece, piece), :]
                    value = codes.astype(jnp.int32).astype(F32) * scales
                acc, place = (accq, place_q) if which == "q" else (accd, place_d)
                rows = pl.ds(place(into) * c + p * piece, piece)
                acc[rows, :] = acc[rows, :] + value
                if into and stage_of(slot) == stage_of(into) + 1:
                    send(which, into, p)

    def grad_q(slots):
        for slot in slots:
            rows = pl.ds(place_q(slot) * c, pair)
            accq[rows, :] = lax.dot_general(
                wts[:, rows], dall[...], (((0,), (0,)), ((), ())), preferred_element_type=F32
            )
            for p in range(PIECES):
                send("q", slot + half, p)

    def grad_d(slots):
        for slot in slots:
            rows = pl.ds(place_d(slot) * c, pair)
            accd[rows, :] = jnp.dot(wts[rows, :], qall[...], preferred_element_type=F32)
            for p in range(PIECES):
                send("d", slot + nd // 2, p)

    early_q, late_q = falling(half, half // 2), falling(half // 2, 0)
    for slot in falling(nd // 2, nd // 4):
        weigh([place_d(slot), place_d(slot) + 1])
        grad_d([slot])
    for slot in falling(nd // 4, 0):
        weigh([place_d(slot), place_d(slot) + 1])
    grad_q(early_q)
    absorb("q", [early_q[0] + half])
    grad_d(falling(nd // 4, 0))
    absorb("q", [slot + half for slot in early_q[1:]])
    grad_q(late_q)
    for copy in loss_copies:
        copy.start()

    absorb("d", falling(nd, 3 * nd // 4))
    absorb("q", [slot + half for slot in late_q])
    rest_q, rest_d = falling(half, 1), falling(3 * nd // 4, 1)
    for i in range(max(len(rest_q), len(rest_d))):
        absorb("q", rest_q[i:i + 1])
        absorb("d", rest_d[i:i + 1])

    own = pl.ds(0, c)
    stores = [
        pltpu.make_async_copy(accq.at[own, :], outq_ref, io_sem.at[3]),
        pltpu.make_async_copy(accd.at[own, :], outd_ref, io_sem.at[4]),
    ]
    accq[own, :] = project(20.0 * accq[own, :], *normalize(qown[...]))
    stores[0].start()
    accd[own, :] = project(20.0 * accd[own, :], *normalize(down[...]))
    stores[1].start()

    for copy in loss_copies:
        copy.wait_recv()
    row = tree_sum([losses[k] for k in range(nd)])
    loss_ref[...] = jnp.sum(row, axis=1, keepdims=True) / (c * n)

    for p in range(PIECES):
        for slot in range(1, nq):
            gq(slot, p).wait_send()
            for copy in nq_copies(slot, p) if slot < half else (wide_copy(slot, p),):
                copy.wait_send()
        for slot in range(1, nd):
            gd(slot, p).wait_send()
            for copy in nd_copies(slot, p):
                copy.wait_send()
    for copy in pos_copies + stat_copies + loss_copies:
        copy.wait_send()
    for copy in stores:
        copy.wait()


def hand_over(sumq_ref, sumd_ref, outq_ref, outd_ref, stage, sem):
    rows = sumq_ref.shape[0] // 2
    parts = [
        (ref.at[pl.ds(h * rows, rows), :], out.at[pl.ds(h * rows, rows), :])
        for ref, out in ((sumq_ref, outq_ref), (sumd_ref, outd_ref)) for h in range(2)
    ]
    loads = [
        pltpu.make_async_copy(ref, stage.at[i], sem.at[0, i]) for i, (ref, out) in enumerate(parts)
    ]
    stores = [
        pltpu.make_async_copy(stage.at[i], out, sem.at[1, i]) for i, (ref, out) in enumerate(parts)
    ]
    for copy in loads:
        copy.start()
    for load, store in zip(loads, stores):
        load.wait()
        store.start()
    for copy in stores:
        copy.wait()


def local(queries, documents, positives):
    n = lax.axis_size("dp")
    c, width = queries.shape
    qbits, dbits = group_bits(n)
    nq, nd = 1 << len(qbits), 1 << len(dbits)
    dma = pltpu.SemaphoreType.DMA
    vmem = pl.BlockSpec(memory_space=pltpu.VMEM)
    tile = jax.ShapeDtypeStruct((c, width), F32)
    anywhere = pl.BlockSpec(memory_space=pl.ANY)
    buffers = [
        ((c, width), BF16),
        ((c, width), BF16),
        ((nq * c, width), BF16),
        ((nd * c, width), BF16),
        ((1, nq * c), jnp.int32),
        ((nd * c, nq * c), F32),
        ((nd * c, nq * c), BF16),
        ((nq, 2, nq * c), F32),
        ((nd, 1, c), F32),
        ((nq * c, width), F32),
        ((nd * c, width), F32),
        ((nq // 2 * c, width), F32),
        ((nq // 2 * c, width), jnp.int16),
        ((nq // 2 * c, width), jnp.int16),
        ((nd * c, width), jnp.int16),
        ((nd * c, width), jnp.int16),
        ((nq // 2 * PIECES, 1, 128), F32),
        ((nq // 2 * PIECES, 1, 128), F32),
        ((nd * PIECES, 1, 128), F32),
        ((nd * PIECES, 1, 128), F32),
    ]
    loss, grad_q, grad_d = pl.pallas_call(
        functools.partial(kernel, n, qbits, dbits),
        out_shape=(jax.ShapeDtypeStruct((1, 1), F32), tile, tile),
        in_specs=[anywhere] * 3,
        out_specs=(vmem, anywhere, anywhere),
        scratch_shapes=[pltpu.VMEM(shape, kind) for shape, kind in buffers] + [
            dma((nq, PIECES)), dma((nq, PIECES)), dma((nd, PIECES)), dma((nd, PIECES)),
            dma((nq,)), dma((nq,)), dma((nq,)), dma((nq,)), dma((nd,)), dma((nd,)),
            dma((nq, PIECES)), dma((nq, PIECES)), dma((nd, PIECES)), dma((nd, PIECES)),
            dma((nq, PIECES)), dma((nq, PIECES)), dma((nd, PIECES)), dma((nd, PIECES)),
            dma((5,)),
        ],
        compiler_params=pltpu.CompilerParams(
            collective_id=0, has_side_effects=True,
            vmem_limit_bytes=VMEM_BYTES,
        ),
        cost_estimate=pl.CostEstimate(
            flops=6 * nq * c * nd * c * width,
            bytes_accessed=12 * c * width,
            transcendentals=nq * c * nd * c,
        ),
    )(queries, documents, positives.reshape(1, c))
    grad_q, grad_d = pl.pallas_call(
        hand_over,
        out_shape=(tile, tile),
        in_specs=[anywhere] * 2,
        out_specs=(anywhere, anywhere),
        scratch_shapes=[pltpu.VMEM((4, c // 2, width), F32), dma((2, 4))],
        compiler_params=pltpu.CompilerParams(vmem_limit_bytes=VMEM_BYTES),
        cost_estimate=pl.CostEstimate(
            flops=0, bytes_accessed=16 * c * width, transcendentals=0
        ),
    )(grad_q, grad_d)
    return (loss.reshape(()), grad_q, grad_d)


def solution(mesh):
    placed = (P("dp", None), P("dp", None), P("dp"))
    return jax.shard_map(
        local,
        mesh=mesh,
        in_specs=placed,
        out_specs=(P(), P("dp", None), P("dp", None)),
        check_vma=False,
    )
```

```python
import functools

import jax
import jax.numpy as jnp
from jax import lax
from jax.experimental import pallas as pl
from jax.experimental.pallas import tpu as pltpu
from jax.sharding import PartitionSpec as P

PIECES = 2
VMEM_BYTES = 56 << 20
F32 = jnp.float32
BF16 = jnp.bfloat16


def tree_sum(terms):
    while len(terms) > 1:
        terms = [terms[i] + terms[i + 1] for i in range(0, len(terms), 2)]
    return terms[0]


def normalize(values):
    wide = values.astype(F32)
    length = jnp.sqrt(jnp.sum(wide * wide, axis=1, keepdims=True) + 1e-06)
    return wide / length, length


def project(grad, unit, length):
    return (grad - jnp.sum(grad * unit, axis=1, keepdims=True) * unit) / length


def group_bits(n):
    bits = n.bit_length() - 1
    odd = [b for b in range(bits - 1, 0, -1) if b % 2 == 1]
    even = [b for b in range(bits - 1, 0, -1) if b % 2 == 0]
    return odd + [0], even


def stage_of(slot):
    return slot.bit_length() - 1


def place_of(slot, bits):
    return sum(((slot >> j) & 1) << (len(bits) - 1 - j) for j in range(len(bits)))


def falling(high, low):
    return list(range(high - 1, low - 1, -1))


def kernel(
    n, qbits, dbits,
    q_ref, d_ref, pos_ref,
    loss_ref, outq_ref, outd_ref,
    qown, down, qall, dall, posrow, expd, wts, stats, losses, accq, accd, wideq,
    codeq, gotq, coded, gotd, scaleq, gotsq, scaled, gotsd,
    qs_sem, qr_sem, ds_sem, dr_sem, ps_sem, pr_sem, ss_sem, sr_sem, ls_sem, lr_sem,
    aqs_sem, aqr_sem, ads_sem, adr_sem, cqs_sem, cqr_sem, cds_sem, cdr_sem, io_sem,
):
    me = lax.axis_index("dp")
    c, width = q_ref.shape
    piece = c // PIECES
    nq, nd = 1 << len(qbits), 1 << len(dbits)
    half = nq // 2

    def flipped(bits, slot):
        where = me
        for j, b in enumerate(bits):
            if (slot >> j) & 1:
                where = where + (1 - 2 * (lax.rem(lax.div(me, 1 << b), 2))) * (1 << b)
        return where

    def place_q(slot):
        return place_of(slot, qbits)

    def place_d(slot):
        return place_of(slot, dbits)

    peer_q = [flipped(qbits, k) for k in range(nq)]
    peer_d = [flipped(dbits, k) for k in range(nd)]

    loads = [
        pltpu.make_async_copy(q_ref, qown, io_sem.at[0]),
        pltpu.make_async_copy(d_ref, down, io_sem.at[1]),
        pltpu.make_async_copy(pos_ref, posrow.at[:, pl.ds(0, c)], io_sem.at[2]),
    ]
    for copy in loads:
        copy.start()
    barrier = pltpu.get_barrier_semaphore()
    for peer in peer_q[1:] + peer_d[1:]:
        pl.semaphore_signal(barrier, inc=1, device_id=(peer,), device_id_type=pl.DeviceIdType.MESH)

    for copy in loads:
        copy.wait()
    qall[pl.ds(0, c), :] = normalize(qown[...])[0].astype(BF16)
    dall[pl.ds(0, c), :] = normalize(down[...])[0].astype(BF16)

    pl.semaphore_wait(barrier, nq + nd - 2)

    def remote(src, dst, send, recv, peer):
        return pltpu.make_async_remote_copy(
            src_ref=src, dst_ref=dst, send_sem=send, recv_sem=recv,
            device_id=(peer,), device_id_type=pl.DeviceIdType.MESH,
        )

    def gather_copy(buf, place, send, recv, peers, slot, p):
        low = slot - (1 << stage_of(slot))
        return remote(
            buf.at[pl.ds(place(low) * c + p * piece, piece), :],
            buf.at[pl.ds(place(slot) * c + p * piece, piece), :],
            send.at[slot, p], recv.at[slot, p], peers[1 << stage_of(slot)],
        )

    gq = functools.partial(gather_copy, qall, place_q, qs_sem, qr_sem, peer_q)
    gd = functools.partial(gather_copy, dall, place_d, ds_sem, dr_sem, peer_d)
    pos_copies = [
        remote(posrow.at[:, pl.ds(0, c)], posrow.at[:, pl.ds(place_q(k) * c, c)],
               ps_sem.at[k], pr_sem.at[k], peer_q[k])
        for k in range(1, nq)
    ]

    for p in range(PIECES):
        for j in range(len(qbits)):
            gq(1 << j, p).start()
            if j < len(dbits):
                gd(1 << j, p).start()
    for copy in pos_copies:
        copy.start()

    def arrive(make, bits, slots):
        for slot in slots:
            for p in range(PIECES):
                make(slot, p).wait_recv()
                for j in range(stage_of(slot) + 1, len(bits)):
                    make(slot + (1 << j), p).start()

    pair = 2 * c
    bases = [peer_d[place_d(i)] * c for i in range(nd)]

    def hits(j, i):
        start = j * pair if isinstance(j, int) else pl.multiple_of(j * pair, pair)
        return lax.broadcasted_iota(jnp.int32, (c, pair), 0) == posrow[:, pl.ds(start, pair)] - bases[i]

    def score(pairs, first, last):

        def step(j, carry):
            lanes = pl.ds(pl.multiple_of(j * pair, pair), pair)
            if first:
                total, picked = stats[0, 0:1, lanes], stats[0, 1:2, lanes]
            else:
                total, picked = jnp.zeros((1, pair), F32), jnp.zeros((1, pair), F32)
            dots = lax.dot_general(
                dall[pl.ds(first * c, (last - first) * c), :], qall[lanes, :],
                (((1,), (1,)), ((), ())), preferred_element_type=F32,
            )
            for i in range(first, last):
                scores = 20.0 * dots[(i - first) * c:(i - first + 1) * c, :]
                powers = jnp.exp(scores - 20.0)
                expd[pl.ds(i * c, c), lanes] = powers
                total = total + jnp.sum(powers, axis=0, keepdims=True)
                picked = picked + jnp.sum(
                    jnp.where(hits(j, i), scores, 0.0), axis=0, keepdims=True
                )
            stats[0, 0:1, lanes] = total
            stats[0, 1:2, lanes] = picked
            return carry

        lax.fori_loop(pairs[0], pairs[1], step, 0, unroll=True)

    arrive(gq, qbits, [1])
    arrive(gq, qbits, range(2, nq, 2))
    arrive(gd, dbits, range(2, nd, 2))
    for copy in pos_copies:
        copy.wait_recv()
    low, high = nd // 2, 3 * nd // 4
    score((0, nq // 4), 0, low)
    arrive(gd, dbits, [1])
    arrive(gq, qbits, [3])
    arrive(gq, qbits, range(5, nq, 4))
    arrive(gd, dbits, range(5, nd, 4))
    score((nq // 4, 3 * nq // 8), 0, low)
    score((0, 3 * nq // 8), low, high)
    arrive(gq, qbits, range(7, nq, 4))
    score((3 * nq // 8, nq // 2), 0, high)
    arrive(gd, dbits, range(3, nd, 4))
    score((0, nq // 2), high, nd)

    stat_copies = [
        remote(stats.at[0], stats.at[k], ss_sem.at[k], sr_sem.at[k], peer_q[k])
        for k in range(1, nq)
    ]
    for copy in stat_copies:
        copy.start()
    for p in range(PIECES):
        for slot in range(1, nq):
            gq(slot, p).wait_send()
        for slot in range(1, nd):
            gd(slot, p).wait_send()
    for copy in pos_copies:
        copy.wait_send()
    for copy in stat_copies:
        copy.wait_recv()

    def slot_total(row, r):
        return tree_sum(
            [stats[k, row:row + 1, pl.ds(place_q(r ^ k) * c, c)] for k in range(nq)]
        )

    totals = [slot_total(0, r) for r in range(nq)]
    losses[0] = tree_sum([20.0 + jnp.log(totals[r]) - slot_total(1, r) for r in range(nq)])
    loss_copies = [
        remote(losses.at[0], losses.at[k], ls_sem.at[k], lr_sem.at[k], peer_d[k])
        for k in range(1, nd)
    ]

    inverses = [
        1.0 / jnp.concatenate([totals[place_q(2 * j)], totals[place_q(2 * j + 1)]], axis=1)
        for j in range(nq // 2)
    ]

    def weigh(places):
        for i in places:
            rows = pl.ds(i * c, c)
            for j in range(nq // 2):
                lanes = pl.ds(j * pair, pair)
                hit = jnp.where(hits(j, i), 1.0, 0.0)
                wts[rows, lanes] = (expd[rows, lanes] * inverses[j] - hit).astype(BF16)

    diagonal = lax.broadcasted_iota(jnp.int32, (piece, 128), 0) == lax.broadcasted_iota(
        jnp.int32, (piece, 128), 1
    )

    def narrow_copies(code, got, scale, gots, sems, peers, slot, p):
        rows = pl.ds(slot * c + p * piece, piece)
        line = slot * PIECES + p
        peer = peers[1 << stage_of(slot)]
        return (
            remote(code.at[rows, :], got.at[rows, :], sems[0].at[slot, p], sems[1].at[slot, p], peer),
            remote(scale.at[line], gots.at[line], sems[2].at[slot, p], sems[3].at[slot, p], peer),
        )

    nq_copies = functools.partial(
        narrow_copies, codeq, gotq, scaleq, gotsq, (aqs_sem, aqr_sem, cqs_sem, cqr_sem), peer_q
    )
    nd_copies = functools.partial(
        narrow_copies, coded, gotd, scaled, gotsd, (ads_sem, adr_sem, cds_sem, cdr_sem), peer_d
    )

    def wide_copy(slot, p):
        return remote(
            accq.at[pl.ds(place_q(slot) * c + p * piece, piece), :],
            wideq.at[pl.ds((slot - half) * c + p * piece, piece), :],
            aqs_sem.at[slot, p], aqr_sem.at[slot, p], peer_q[half],
        )

    def pack(which, slot, p):
        acc, place, code, scale = (
            (accq, place_q, codeq, scaleq) if which == "q" else (accd, place_d, coded, scaled)
        )
        value = acc[pl.ds(place(slot) * c + p * piece, piece), :]
        top = jnp.maximum(jnp.max(jnp.abs(value), axis=1, keepdims=True), 1e-30)
        codes = jnp.round(value * (32767.0 / top))
        code[pl.ds(slot * c + p * piece, piece), :] = codes.astype(jnp.int32).astype(jnp.int16)
        scale[slot * PIECES + p] = jnp.sum(
            jnp.where(diagonal, top * (1.0 / 32767.0), 0.0), axis=0, keepdims=True
        )

    def copies_of(which, slot, p):
        if which == "q" and slot >= half:
            return (wide_copy(slot, p),)
        return nq_copies(slot, p) if which == "q" else nd_copies(slot, p)

    def send(which, slot, pieces=range(PIECES)):
        if which == "d" or slot < half:
            for p in pieces:
                pack(which, slot, p)
        for p in pieces:
            for copy in copies_of(which, slot, p):
                copy.start()

    def add(which, slot, p):
        into = slot - (1 << stage_of(slot))
        if which == "q" and slot >= half:
            value = wideq[pl.ds((slot - half) * c + p * piece, piece), :]
        else:
            got, gots = (gotq, gotsq) if which == "q" else (gotd, gotsd)
            scales = jnp.sum(
                jnp.where(diagonal, gots[slot * PIECES + p], 0.0), axis=1, keepdims=True
            )
            codes = got[pl.ds(slot * c + p * piece, piece), :]
            value = codes.astype(jnp.int32).astype(F32) * scales
        acc, place = (accq, place_q) if which == "q" else (accd, place_d)
        rows = pl.ds(place(into) * c + p * piece, piece)
        acc[rows, :] = acc[rows, :] + value

    def absorb(which, slots):
        for slot in slots:
            into = slot - (1 << stage_of(slot))
            onward = into > 0 and stage_of(slot) == stage_of(into) + 1
            groups = [[p] for p in range(PIECES)] if onward else [range(PIECES)]
            for pieces in groups:
                for p in pieces:
                    for copy in copies_of(which, slot, p):
                        copy.wait_recv()
                for p in pieces:
                    add(which, slot, p)
                if onward:
                    send(which, into, pieces)

    def grad_q(slots):
        for slot in slots:
            rows = pl.ds(place_q(slot) * c, pair)
            accq[rows, :] = lax.dot_general(
                wts[:, rows], dall[...], (((0,), (0,)), ((), ())), preferred_element_type=F32
            )
            send("q", slot + half)

    def grad_d(slots):
        for slot in slots:
            rows = pl.ds(place_d(slot) * c, pair)
            accd[rows, :] = jnp.dot(wts[rows, :], qall[...], preferred_element_type=F32)
            send("d", slot + nd // 2)

    early_q, late_q = falling(half, half // 2), falling(half // 2, 0)
    for slot in falling(nd // 2, nd // 4):
        weigh([place_d(slot), place_d(slot) + 1])
        grad_d([slot])
    for slot in falling(nd // 4, 0):
        weigh([place_d(slot), place_d(slot) + 1])
    grad_q(early_q)
    absorb("q", [early_q[0] + half])
    grad_d(falling(nd // 4, 0))
    absorb("d", falling(nd, 3 * nd // 4))
    absorb("q", [slot + half for slot in early_q[1:]])
    grad_q(late_q)
    for copy in loss_copies:
        copy.start()

    absorb("q", [slot + half for slot in late_q])
    for p in range(PIECES):
        for slot in range(half, nq):
            wide_copy(slot, p).wait_send()
    for copy in stat_copies:
        copy.wait_send()
    rest_q, rest_d = falling(half, 1), falling(3 * nd // 4, 1)
    for i in range(max(len(rest_q), len(rest_d))):
        absorb("q", rest_q[i:i + 1])
        absorb("d", rest_d[i:i + 1])

    own = pl.ds(0, c)
    stores = [
        pltpu.make_async_copy(accq.at[own, :], outq_ref, io_sem.at[3]),
        pltpu.make_async_copy(accd.at[own, :], outd_ref, io_sem.at[4]),
    ]
    accq[own, :] = project(20.0 * accq[own, :], *normalize(qown[...]))
    stores[0].start()
    accd[own, :] = project(20.0 * accd[own, :], *normalize(down[...]))
    stores[1].start()

    for copy in loss_copies:
        copy.wait_recv()
    row = tree_sum([losses[k] for k in range(nd)])
    loss_ref[...] = jnp.sum(row, axis=1, keepdims=True) / (c * n)

    for p in range(PIECES):
        for slot in range(1, half):
            for copy in nq_copies(slot, p):
                copy.wait_send()
        for slot in range(1, nd):
            for copy in nd_copies(slot, p):
                copy.wait_send()
    for copy in loss_copies:
        copy.wait_send()
    for copy in stores:
        copy.wait()


def hand_over(sumq_ref, sumd_ref, outq_ref, outd_ref, stage, sem):
    rows = sumq_ref.shape[0] // 2
    parts = [
        (ref.at[pl.ds(h * rows, rows), :], out.at[pl.ds(h * rows, rows), :])
        for ref, out in ((sumq_ref, outq_ref), (sumd_ref, outd_ref)) for h in range(2)
    ]
    loads = [
        pltpu.make_async_copy(ref, stage.at[i], sem.at[0, i]) for i, (ref, out) in enumerate(parts)
    ]
    stores = [
        pltpu.make_async_copy(stage.at[i], out, sem.at[1, i]) for i, (ref, out) in enumerate(parts)
    ]
    for copy in loads:
        copy.start()
    for load, store in zip(loads, stores):
        load.wait()
        store.start()
    for copy in stores:
        copy.wait()


def local(queries, documents, positives):
    n = lax.axis_size("dp")
    c, width = queries.shape
    qbits, dbits = group_bits(n)
    nq, nd = 1 << len(qbits), 1 << len(dbits)
    dma = pltpu.SemaphoreType.DMA
    vmem = pl.BlockSpec(memory_space=pltpu.VMEM)
    tile = jax.ShapeDtypeStruct((c, width), F32)
    anywhere = pl.BlockSpec(memory_space=pl.ANY)
    buffers = [
        ((c, width), BF16),
        ((c, width), BF16),
        ((nq * c, width), BF16),
        ((nd * c, width), BF16),
        ((1, nq * c), jnp.int32),
        ((nd * c, nq * c), F32),
        ((nd * c, nq * c), BF16),
        ((nq, 2, nq * c), F32),
        ((nd, 1, c), F32),
        ((nq * c, width), F32),
        ((nd * c, width), F32),
        ((nq // 2 * c, width), F32),
        ((nq // 2 * c, width), jnp.int16),
        ((nq // 2 * c, width), jnp.int16),
        ((nd * c, width), jnp.int16),
        ((nd * c, width), jnp.int16),
        ((nq // 2 * PIECES, 1, 128), F32),
        ((nq // 2 * PIECES, 1, 128), F32),
        ((nd * PIECES, 1, 128), F32),
        ((nd * PIECES, 1, 128), F32),
    ]
    loss, grad_q, grad_d = pl.pallas_call(
        functools.partial(kernel, n, qbits, dbits),
        out_shape=(jax.ShapeDtypeStruct((1, 1), F32), tile, tile),
        in_specs=[anywhere] * 3,
        out_specs=(vmem, anywhere, anywhere),
        scratch_shapes=[pltpu.VMEM(shape, kind) for shape, kind in buffers] + [
            dma((nq, PIECES)), dma((nq, PIECES)), dma((nd, PIECES)), dma((nd, PIECES)),
            dma((nq,)), dma((nq,)), dma((nq,)), dma((nq,)), dma((nd,)), dma((nd,)),
            dma((nq, PIECES)), dma((nq, PIECES)), dma((nd, PIECES)), dma((nd, PIECES)),
            dma((nq, PIECES)), dma((nq, PIECES)), dma((nd, PIECES)), dma((nd, PIECES)),
            dma((5,)),
        ],
        compiler_params=pltpu.CompilerParams(
            collective_id=0, has_side_effects=True,
            vmem_limit_bytes=VMEM_BYTES,
        ),
        cost_estimate=pl.CostEstimate(
            flops=6 * nq * c * nd * c * width,
            bytes_accessed=12 * c * width,
            transcendentals=nq * c * nd * c,
        ),
    )(queries, documents, positives.reshape(1, c))
    grad_q, grad_d = pl.pallas_call(
        hand_over,
        out_shape=(tile, tile),
        in_specs=[anywhere] * 2,
        out_specs=(anywhere, anywhere),
        scratch_shapes=[pltpu.VMEM((4, c // 2, width), F32), dma((2, 4))],
        compiler_params=pltpu.CompilerParams(vmem_limit_bytes=VMEM_BYTES),
        cost_estimate=pl.CostEstimate(
            flops=0, bytes_accessed=16 * c * width, transcendentals=0
        ),
    )(grad_q, grad_d)
    return (loss.reshape(()), grad_q, grad_d)


def solution(mesh):
    placed = (P("dp", None), P("dp", None), P("dp"))
    return jax.shard_map(
        local,
        mesh=mesh,
        in_specs=placed,
        out_specs=(P(), P("dp", None), P("dp", None)),
        check_vma=False,
    )
```

```python
import functools

import jax
import jax.numpy as jnp
from jax import lax
from jax.experimental import pallas as pl
from jax.experimental.pallas import tpu as pltpu
from jax.sharding import PartitionSpec as P

PIECES = 2
SHARD_PIECES = 4
VMEM_BYTES = 56 << 20
F32 = jnp.float32
BF16 = jnp.bfloat16


def tree_sum(terms):
    while len(terms) > 1:
        terms = [terms[i] + terms[i + 1] for i in range(0, len(terms), 2)]
    return terms[0]


def normalize(values):
    wide = values.astype(F32)
    length = jnp.sqrt(jnp.sum(wide * wide, axis=1, keepdims=True) + 1e-06)
    return wide / length, length


def project(grad, unit, length):
    return (grad - jnp.sum(grad * unit, axis=1, keepdims=True) * unit) / length


def group_bits(n):
    bits = n.bit_length() - 1
    odd = [b for b in range(bits - 1, 0, -1) if b % 2 == 1]
    even = [b for b in range(bits - 1, 0, -1) if b % 2 == 0]
    return odd + [0], even


def stage_of(slot):
    return slot.bit_length() - 1


def place_of(slot, bits):
    return sum(((slot >> j) & 1) << (len(bits) - 1 - j) for j in range(len(bits)))


def falling(high, low):
    return list(range(high - 1, low - 1, -1))


def kernel(
    n, qbits, dbits,
    q_ref, d_ref, pos_ref,
    loss_ref, outq_ref, outd_ref,
    qown, down, qall, dall, posrow, expd, wts, stats, losses, accq, accd, wideq,
    codeq, gotq, coded, gotd, scaleq, gotsq, scaled, gotsd,
    qs_sem, qr_sem, ds_sem, dr_sem, ps_sem, pr_sem, ss_sem, sr_sem, ls_sem, lr_sem,
    aqs_sem, aqr_sem, ads_sem, adr_sem, cqs_sem, cqr_sem, cds_sem, cdr_sem, io_sem,
):
    me = lax.axis_index("dp")
    c, width = q_ref.shape
    piece, part = c // PIECES, c // SHARD_PIECES
    nq, nd = 1 << len(qbits), 1 << len(dbits)
    half = nq // 2

    def flipped(bits, slot):
        where = me
        for j, b in enumerate(bits):
            if (slot >> j) & 1:
                where = where + (1 - 2 * (lax.rem(lax.div(me, 1 << b), 2))) * (1 << b)
        return where

    def place_q(slot):
        return place_of(slot, qbits)

    def place_d(slot):
        return place_of(slot, dbits)

    peer_q = [flipped(qbits, k) for k in range(nq)]
    peer_d = [flipped(dbits, k) for k in range(nd)]

    loads = [
        pltpu.make_async_copy(q_ref, qown, io_sem.at[0]),
        pltpu.make_async_copy(d_ref, down, io_sem.at[1]),
        pltpu.make_async_copy(pos_ref, posrow.at[:, pl.ds(0, c)], io_sem.at[2]),
    ]
    for copy in loads:
        copy.start()
    barrier = pltpu.get_barrier_semaphore()
    for peer in peer_q[1:] + peer_d[1:]:
        pl.semaphore_signal(barrier, inc=1, device_id=(peer,), device_id_type=pl.DeviceIdType.MESH)

    for copy in loads:
        copy.wait()
    qall[pl.ds(0, c), :] = normalize(qown[...])[0].astype(BF16)
    dall[pl.ds(0, c), :] = normalize(down[...])[0].astype(BF16)

    pl.semaphore_wait(barrier, nq + nd - 2)

    def remote(src, dst, send, recv, peer):
        return pltpu.make_async_remote_copy(
            src_ref=src, dst_ref=dst, send_sem=send, recv_sem=recv,
            device_id=(peer,), device_id_type=pl.DeviceIdType.MESH,
        )

    def gather_copy(buf, place, send, recv, peers, slot, p):
        low = slot - (1 << stage_of(slot))
        return remote(
            buf.at[pl.ds(place(low) * c + p * part, part), :],
            buf.at[pl.ds(place(slot) * c + p * part, part), :],
            send.at[slot, p], recv.at[slot, p], peers[1 << stage_of(slot)],
        )

    gq = functools.partial(gather_copy, qall, place_q, qs_sem, qr_sem, peer_q)
    gd = functools.partial(gather_copy, dall, place_d, ds_sem, dr_sem, peer_d)
    pos_copies = [
        remote(posrow.at[:, pl.ds(0, c)], posrow.at[:, pl.ds(place_q(k) * c, c)],
               ps_sem.at[k], pr_sem.at[k], peer_q[k])
        for k in range(1, nq)
    ]

    for p in range(SHARD_PIECES):
        for j in range(len(qbits)):
            gq(1 << j, p).start()
            if j < len(dbits):
                gd(1 << j, p).start()
    for copy in pos_copies:
        copy.start()

    def arrive(make, bits, slots):
        for slot in slots:
            for p in range(SHARD_PIECES):
                make(slot, p).wait_recv()
                for j in range(stage_of(slot) + 1, len(bits)):
                    make(slot + (1 << j), p).start()

    pair = 2 * c
    bases = [peer_d[place_d(i)] * c for i in range(nd)]

    def hits(j, i):
        start = j * pair if isinstance(j, int) else pl.multiple_of(j * pair, pair)
        return lax.broadcasted_iota(jnp.int32, (c, pair), 0) == posrow[:, pl.ds(start, pair)] - bases[i]

    def score(pairs, first, last):

        def step(j, carry):
            lanes = pl.ds(pl.multiple_of(j * pair, pair), pair)
            if first:
                total, picked = stats[0, 0:1, lanes], stats[0, 1:2, lanes]
            else:
                total, picked = jnp.zeros((1, pair), F32), jnp.zeros((1, pair), F32)
            dots = lax.dot_general(
                dall[pl.ds(first * c, (last - first) * c), :], qall[lanes, :],
                (((1,), (1,)), ((), ())), preferred_element_type=F32,
            )
            for i in range(first, last):
                scores = 20.0 * dots[(i - first) * c:(i - first + 1) * c, :]
                powers = jnp.exp(scores - 20.0)
                expd[pl.ds(i * c, c), lanes] = powers
                total = total + jnp.sum(powers, axis=0, keepdims=True)
                picked = picked + jnp.sum(
                    jnp.where(hits(j, i), scores, 0.0), axis=0, keepdims=True
                )
            stats[0, 0:1, lanes] = total
            stats[0, 1:2, lanes] = picked
            return carry

        lax.fori_loop(pairs[0], pairs[1], step, 0, unroll=True)

    arrive(gq, qbits, [1])
    arrive(gq, qbits, range(2, nq, 2))
    arrive(gd, dbits, range(2, nd, 2))
    for copy in pos_copies:
        copy.wait_recv()
    low, high = nd // 2, 3 * nd // 4
    score((0, nq // 4), 0, low)
    arrive(gd, dbits, [1])
    arrive(gq, qbits, [3])
    arrive(gq, qbits, range(5, nq, 4))
    arrive(gd, dbits, range(5, nd, 4))
    score((nq // 4, 3 * nq // 8), 0, low)
    score((0, 3 * nq // 8), low, high)
    arrive(gq, qbits, range(7, nq, 4))
    score((3 * nq // 8, nq // 2), 0, high)
    arrive(gd, dbits, range(3, nd, 4))
    score((0, nq // 2), high, nd)

    stat_copies = [
        remote(stats.at[0], stats.at[k], ss_sem.at[k], sr_sem.at[k], peer_q[k])
        for k in range(1, nq)
    ]
    for copy in stat_copies:
        copy.start()
    for copy in stat_copies:
        copy.wait_recv()

    def slot_total(row, r):
        return tree_sum(
            [stats[k, row:row + 1, pl.ds(place_q(r ^ k) * c, c)] for k in range(nq)]
        )

    totals = [slot_total(0, r) for r in range(nq)]
    losses[0] = tree_sum([20.0 + jnp.log(totals[r]) - slot_total(1, r) for r in range(nq)])
    loss_copies = [
        remote(losses.at[0], losses.at[k], ls_sem.at[k], lr_sem.at[k], peer_d[k])
        for k in range(1, nd)
    ]

    inverses = [
        1.0 / jnp.concatenate([totals[place_q(2 * j)], totals[place_q(2 * j + 1)]], axis=1)
        for j in range(nq // 2)
    ]

    def weigh(places):
        for i in places:
            rows = pl.ds(i * c, c)
            for j in range(nq // 2):
                lanes = pl.ds(j * pair, pair)
                hit = jnp.where(hits(j, i), 1.0, 0.0)
                wts[rows, lanes] = (expd[rows, lanes] * inverses[j] - hit).astype(BF16)

    diagonal = lax.broadcasted_iota(jnp.int32, (piece, 128), 0) == lax.broadcasted_iota(
        jnp.int32, (piece, 128), 1
    )

    def narrow_copies(code, got, scale, gots, sems, peers, slot, p):
        rows = pl.ds(slot * c + p * piece, piece)
        line = slot * PIECES + p
        peer = peers[1 << stage_of(slot)]
        return (
            remote(code.at[rows, :], got.at[rows, :], sems[0].at[slot, p], sems[1].at[slot, p], peer),
            remote(scale.at[line], gots.at[line], sems[2].at[slot, p], sems[3].at[slot, p], peer),
        )

    nq_copies = functools.partial(
        narrow_copies, codeq, gotq, scaleq, gotsq, (aqs_sem, aqr_sem, cqs_sem, cqr_sem), peer_q
    )
    nd_copies = functools.partial(
        narrow_copies, coded, gotd, scaled, gotsd, (ads_sem, adr_sem, cds_sem, cdr_sem), peer_d
    )

    def wide_copy(slot, p):
        return remote(
            accq.at[pl.ds(place_q(slot) * c + p * piece, piece), :],
            wideq.at[pl.ds((slot - half) * c + p * piece, piece), :],
            aqs_sem.at[slot, p], aqr_sem.at[slot, p], peer_q[half],
        )

    def send(which, slot, p):
        if which == "q" and slot >= half:
            wide_copy(slot, p).start()
            return
        acc, place, code, scale, copies = (
            (accq, place_q, codeq, scaleq, nq_copies) if which == "q"
            else (accd, place_d, coded, scaled, nd_copies)
        )
        value = acc[pl.ds(place(slot) * c + p * piece, piece), :]
        top = jnp.maximum(jnp.max(jnp.abs(value), axis=1, keepdims=True), 1e-30)
        codes = jnp.round(value * (32767.0 / top))
        code[pl.ds(slot * c + p * piece, piece), :] = codes.astype(jnp.int32).astype(jnp.int16)
        scale[slot * PIECES + p] = jnp.sum(
            jnp.where(diagonal, top * (1.0 / 32767.0), 0.0), axis=0, keepdims=True
        )
        for copy in copies(slot, p):
            copy.start()

    def absorb(which, slots):
        for slot in slots:
            into = slot - (1 << stage_of(slot))
            for p in range(PIECES):
                if which == "q" and slot >= half:
                    wide_copy(slot, p).wait_recv()
                    value = wideq[pl.ds((slot - half) * c + p * piece, piece), :]
                else:
                    got, gots, copies = (
                        (gotq, gotsq, nq_copies) if which == "q" else (gotd, gotsd, nd_copies)
                    )
                    for copy in copies(slot, p):
                        copy.wait_recv()
                    scales = jnp.sum(
                        jnp.where(diagonal, gots[slot * PIECES + p], 0.0), axis=1, keepdims=True
                    )
                    codes = got[pl.ds(slot * c + p * piece, piece), :]
                    value = codes.astype(jnp.int32).astype(F32) * scales
                acc, place = (accq, place_q) if which == "q" else (accd, place_d)
                rows = pl.ds(place(into) * c + p * piece, piece)
                acc[rows, :] = acc[rows, :] + value
                if into and stage_of(slot) == stage_of(into) + 1:
                    send(which, into, p)

    def grad_q(slots):
        for slot in slots:
            rows = pl.ds(place_q(slot) * c, pair)
            accq[rows, :] = lax.dot_general(
                wts[:, rows], dall[...], (((0,), (0,)), ((), ())), preferred_element_type=F32
            )
            for p in range(PIECES):
                send("q", slot + half, p)

    def grad_d(slots):
        for slot in slots:
            rows = pl.ds(place_d(slot) * c, pair)
            accd[rows, :] = jnp.dot(wts[rows, :], qall[...], preferred_element_type=F32)
            for p in range(PIECES):
                send("d", slot + nd // 2, p)

    early_q, late_q = falling(half, half // 2), falling(half // 2, 0)
    for slot in falling(nd // 2, nd // 4):
        weigh([place_d(slot), place_d(slot) + 1])
        grad_d([slot])
    for slot in falling(nd // 4, 0):
        weigh([place_d(slot), place_d(slot) + 1])
    grad_q(early_q)
    absorb("q", [early_q[0] + half])
    grad_d(falling(nd // 4, 0))
    absorb("q", [slot + half for slot in early_q[1:]])
    grad_q(late_q)
    for copy in loss_copies:
        copy.start()

    absorb("d", falling(nd, 3 * nd // 4))
    absorb("q", [slot + half for slot in late_q])
    rest_q, rest_d = falling(half, 1), falling(3 * nd // 4, 1)
    for i in range(max(len(rest_q), len(rest_d))):
        absorb("q", rest_q[i:i + 1])
        absorb("d", rest_d[i:i + 1])

    own = pl.ds(0, c)
    stores = [
        pltpu.make_async_copy(accq.at[own, :], outq_ref, io_sem.at[3]),
        pltpu.make_async_copy(accd.at[own, :], outd_ref, io_sem.at[4]),
    ]
    accq[own, :] = project(20.0 * accq[own, :], *normalize(qown[...]))
    stores[0].start()
    accd[own, :] = project(20.0 * accd[own, :], *normalize(down[...]))
    stores[1].start()

    for copy in loss_copies:
        copy.wait_recv()
    row = tree_sum([losses[k] for k in range(nd)])
    loss_ref[...] = jnp.sum(row, axis=1, keepdims=True) / (c * n)

    for p in range(SHARD_PIECES):
        for slot in range(1, nq):
            gq(slot, p).wait_send()
        for slot in range(1, nd):
            gd(slot, p).wait_send()
    for p in range(PIECES):
        for slot in range(1, nq):
            for copy in nq_copies(slot, p) if slot < half else (wide_copy(slot, p),):
                copy.wait_send()
        for slot in range(1, nd):
            for copy in nd_copies(slot, p):
                copy.wait_send()
    for copy in pos_copies + stat_copies + loss_copies:
        copy.wait_send()
    for copy in stores:
        copy.wait()


def hand_over(sumq_ref, sumd_ref, outq_ref, outd_ref, stage, sem):
    rows = sumq_ref.shape[0] // 2
    parts = [
        (ref.at[pl.ds(h * rows, rows), :], out.at[pl.ds(h * rows, rows), :])
        for ref, out in ((sumq_ref, outq_ref), (sumd_ref, outd_ref)) for h in range(2)
    ]
    loads = [
        pltpu.make_async_copy(ref, stage.at[i], sem.at[0, i]) for i, (ref, out) in enumerate(parts)
    ]
    stores = [
        pltpu.make_async_copy(stage.at[i], out, sem.at[1, i]) for i, (ref, out) in enumerate(parts)
    ]
    for copy in loads:
        copy.start()
    for load, store in zip(loads, stores):
        load.wait()
        store.start()
    for copy in stores:
        copy.wait()


def local(queries, documents, positives):
    n = lax.axis_size("dp")
    c, width = queries.shape
    qbits, dbits = group_bits(n)
    nq, nd = 1 << len(qbits), 1 << len(dbits)
    dma = pltpu.SemaphoreType.DMA
    vmem = pl.BlockSpec(memory_space=pltpu.VMEM)
    tile = jax.ShapeDtypeStruct((c, width), F32)
    anywhere = pl.BlockSpec(memory_space=pl.ANY)
    buffers = [
        ((c, width), BF16),
        ((c, width), BF16),
        ((nq * c, width), BF16),
        ((nd * c, width), BF16),
        ((1, nq * c), jnp.int32),
        ((nd * c, nq * c), F32),
        ((nd * c, nq * c), BF16),
        ((nq, 2, nq * c), F32),
        ((nd, 1, c), F32),
        ((nq * c, width), F32),
        ((nd * c, width), F32),
        ((nq // 2 * c, width), F32),
        ((nq // 2 * c, width), jnp.int16),
        ((nq // 2 * c, width), jnp.int16),
        ((nd * c, width), jnp.int16),
        ((nd * c, width), jnp.int16),
        ((nq // 2 * PIECES, 1, 128), F32),
        ((nq // 2 * PIECES, 1, 128), F32),
        ((nd * PIECES, 1, 128), F32),
        ((nd * PIECES, 1, 128), F32),
    ]
    loss, grad_q, grad_d = pl.pallas_call(
        functools.partial(kernel, n, qbits, dbits),
        out_shape=(jax.ShapeDtypeStruct((1, 1), F32), tile, tile),
        in_specs=[anywhere] * 3,
        out_specs=(vmem, anywhere, anywhere),
        scratch_shapes=[pltpu.VMEM(shape, kind) for shape, kind in buffers] + [
            dma((nq, SHARD_PIECES)), dma((nq, SHARD_PIECES)),
            dma((nd, SHARD_PIECES)), dma((nd, SHARD_PIECES)),
            dma((nq,)), dma((nq,)), dma((nq,)), dma((nq,)), dma((nd,)), dma((nd,)),
            dma((nq, PIECES)), dma((nq, PIECES)), dma((nd, PIECES)), dma((nd, PIECES)),
            dma((nq, PIECES)), dma((nq, PIECES)), dma((nd, PIECES)), dma((nd, PIECES)),
            dma((5,)),
        ],
        compiler_params=pltpu.CompilerParams(
            collective_id=0, has_side_effects=True,
            vmem_limit_bytes=VMEM_BYTES,
        ),
        cost_estimate=pl.CostEstimate(
            flops=6 * nq * c * nd * c * width,
            bytes_accessed=12 * c * width,
            transcendentals=nq * c * nd * c,
        ),
    )(queries, documents, positives.reshape(1, c))
    grad_q, grad_d = pl.pallas_call(
        hand_over,
        out_shape=(tile, tile),
        in_specs=[anywhere] * 2,
        out_specs=(anywhere, anywhere),
        scratch_shapes=[pltpu.VMEM((4, c // 2, width), F32), dma((2, 4))],
        compiler_params=pltpu.CompilerParams(vmem_limit_bytes=VMEM_BYTES),
        cost_estimate=pl.CostEstimate(
            flops=0, bytes_accessed=16 * c * width, transcendentals=0
        ),
    )(grad_q, grad_d)
    return (loss.reshape(()), grad_q, grad_d)


def solution(mesh):
    placed = (P("dp", None), P("dp", None), P("dp"))
    return jax.shard_map(
        local,
        mesh=mesh,
        in_specs=placed,
        out_specs=(P(), P("dp", None), P("dp", None)),
        check_vma=False,
    )
```

```python
import functools

import jax
import jax.numpy as jnp
from jax import lax
from jax.experimental import pallas as pl
from jax.experimental.pallas import tpu as pltpu
from jax.sharding import PartitionSpec as P

PIECES = 2
SHARD_PIECES = 4
VMEM_BYTES = 56 << 20
F32 = jnp.float32
BF16 = jnp.bfloat16


def tree_sum(terms):
    while len(terms) > 1:
        terms = [terms[i] + terms[i + 1] for i in range(0, len(terms), 2)]
    return terms[0]


def normalize(values):
    wide = values.astype(F32)
    length = jnp.sqrt(jnp.sum(wide * wide, axis=1, keepdims=True) + 1e-06)
    return wide / length, length


def project(grad, unit, length):
    return (grad - jnp.sum(grad * unit, axis=1, keepdims=True) * unit) / length


def group_bits(n):
    bits = n.bit_length() - 1
    odd = [b for b in range(bits - 1, 0, -1) if b % 2 == 1]
    even = [b for b in range(bits - 1, 0, -1) if b % 2 == 0]
    return odd + [0], even


def stage_of(slot):
    return slot.bit_length() - 1


def place_of(slot, bits):
    return sum(((slot >> j) & 1) << (len(bits) - 1 - j) for j in range(len(bits)))


def falling(high, low):
    return list(range(high - 1, low - 1, -1))


def kernel(
    n, qbits, dbits,
    q_ref, d_ref, pos_ref,
    loss_ref, outq_ref, outd_ref,
    qown, down, qall, dall, posrow, expd, wts, stats, losses, accq, accd, wideq,
    codeq, gotq, coded, gotd, scaleq, gotsq, scaled, gotsd,
    qs_sem, qr_sem, ds_sem, dr_sem, ps_sem, pr_sem, ss_sem, sr_sem, ls_sem, lr_sem,
    aqs_sem, aqr_sem, ads_sem, adr_sem, cqs_sem, cqr_sem, cds_sem, cdr_sem, io_sem,
):
    me = lax.axis_index("dp")
    c, width = q_ref.shape
    piece, part = c // PIECES, c // SHARD_PIECES
    nq, nd = 1 << len(qbits), 1 << len(dbits)
    half = nq // 2

    def flipped(bits, slot):
        where = me
        for j, b in enumerate(bits):
            if (slot >> j) & 1:
                where = where + (1 - 2 * (lax.rem(lax.div(me, 1 << b), 2))) * (1 << b)
        return where

    def place_q(slot):
        return place_of(slot, qbits)

    def place_d(slot):
        return place_of(slot, dbits)

    peer_q = [flipped(qbits, k) for k in range(nq)]
    peer_d = [flipped(dbits, k) for k in range(nd)]

    loads = [
        pltpu.make_async_copy(q_ref, qown, io_sem.at[0]),
        pltpu.make_async_copy(d_ref, down, io_sem.at[1]),
        pltpu.make_async_copy(pos_ref, posrow.at[:, pl.ds(0, c)], io_sem.at[2]),
    ]
    for copy in loads:
        copy.start()
    barrier = pltpu.get_barrier_semaphore()
    for peer in peer_q[1:] + peer_d[1:]:
        pl.semaphore_signal(barrier, inc=1, device_id=(peer,), device_id_type=pl.DeviceIdType.MESH)

    for copy in loads:
        copy.wait()
    qall[pl.ds(0, c), :] = normalize(qown[...])[0].astype(BF16)
    dall[pl.ds(0, c), :] = normalize(down[...])[0].astype(BF16)

    pl.semaphore_wait(barrier, nq + nd - 2)

    def remote(src, dst, send, recv, peer):
        return pltpu.make_async_remote_copy(
            src_ref=src, dst_ref=dst, send_sem=send, recv_sem=recv,
            device_id=(peer,), device_id_type=pl.DeviceIdType.MESH,
        )

    def gather_copy(buf, place, send, recv, peers, slot, p):
        low = slot - (1 << stage_of(slot))
        return remote(
            buf.at[pl.ds(place(low) * c + p * part, part), :],
            buf.at[pl.ds(place(slot) * c + p * part, part), :],
            send.at[slot, p], recv.at[slot, p], peers[1 << stage_of(slot)],
        )

    gq = functools.partial(gather_copy, qall, place_q, qs_sem, qr_sem, peer_q)
    gd = functools.partial(gather_copy, dall, place_d, ds_sem, dr_sem, peer_d)
    pos_copies = [
        remote(posrow.at[:, pl.ds(0, c)], posrow.at[:, pl.ds(place_q(k) * c, c)],
               ps_sem.at[k], pr_sem.at[k], peer_q[k])
        for k in range(1, nq)
    ]

    for p in range(SHARD_PIECES):
        for j in range(len(qbits)):
            gq(1 << j, p).start()
            if j < len(dbits):
                gd(1 << j, p).start()
    for copy in pos_copies:
        copy.start()

    def arrive(make, bits, slots):
        for slot in slots:
            for p in range(SHARD_PIECES):
                make(slot, p).wait_recv()
                for j in range(stage_of(slot) + 1, len(bits)):
                    make(slot + (1 << j), p).start()

    pair = 2 * c
    bases = [peer_d[place_d(i)] * c for i in range(nd)]

    def hits(j, i):
        start = j * pair if isinstance(j, int) else pl.multiple_of(j * pair, pair)
        return lax.broadcasted_iota(jnp.int32, (c, pair), 0) == posrow[:, pl.ds(start, pair)] - bases[i]

    def score(pairs, first, last):

        def step(j, carry):
            lanes = pl.ds(pl.multiple_of(j * pair, pair), pair)
            if first:
                total, picked = stats[0, 0:1, lanes], stats[0, 1:2, lanes]
            else:
                total, picked = jnp.zeros((1, pair), F32), jnp.zeros((1, pair), F32)
            dots = lax.dot_general(
                dall[pl.ds(first * c, (last - first) * c), :], qall[lanes, :],
                (((1,), (1,)), ((), ())), preferred_element_type=F32,
            )
            for i in range(first, last):
                scores = 20.0 * dots[(i - first) * c:(i - first + 1) * c, :]
                powers = jnp.exp(scores - 20.0)
                expd[pl.ds(i * c, c), lanes] = powers
                total = total + jnp.sum(powers, axis=0, keepdims=True)
                picked = picked + jnp.sum(
                    jnp.where(hits(j, i), scores, 0.0), axis=0, keepdims=True
                )
            stats[0, 0:1, lanes] = total
            stats[0, 1:2, lanes] = picked
            return carry

        lax.fori_loop(pairs[0], pairs[1], step, 0, unroll=True)

    arrive(gq, qbits, [1])
    arrive(gq, qbits, range(2, nq, 2))
    arrive(gd, dbits, range(2, nd, 2))
    for copy in pos_copies:
        copy.wait_recv()
    low, high = nd // 2, 3 * nd // 4
    score((0, nq // 4), 0, low)
    arrive(gd, dbits, [1])
    arrive(gq, qbits, [3])
    arrive(gq, qbits, range(5, nq, 4))
    arrive(gd, dbits, range(5, nd, 4))
    score((nq // 4, 3 * nq // 8), 0, low)
    score((0, 3 * nq // 8), low, high)
    arrive(gq, qbits, range(7, nq, 4))
    score((3 * nq // 8, nq // 2), 0, high)
    arrive(gd, dbits, range(3, nd, 4))
    score((0, nq // 2), high, nd)

    stat_copies = [
        remote(stats.at[0], stats.at[k], ss_sem.at[k], sr_sem.at[k], peer_q[k])
        for k in range(1, nq)
    ]
    for copy in stat_copies:
        copy.start()
    for copy in stat_copies:
        copy.wait_recv()

    def slot_total(row, r):
        return tree_sum(
            [stats[k, row:row + 1, pl.ds(place_q(r ^ k) * c, c)] for k in range(nq)]
        )

    totals = [slot_total(0, r) for r in range(nq)]
    losses[0] = tree_sum([20.0 + jnp.log(totals[r]) - slot_total(1, r) for r in range(nq)])
    loss_copies = [
        remote(losses.at[0], losses.at[k], ls_sem.at[k], lr_sem.at[k], peer_d[k])
        for k in range(1, nd)
    ]

    inverses = [
        1.0 / jnp.concatenate([totals[place_q(2 * j)], totals[place_q(2 * j + 1)]], axis=1)
        for j in range(nq // 2)
    ]

    def weigh(places):
        for i in places:
            rows = pl.ds(i * c, c)
            for j in range(nq // 2):
                lanes = pl.ds(j * pair, pair)
                hit = jnp.where(hits(j, i), 1.0, 0.0)
                wts[rows, lanes] = (expd[rows, lanes] * inverses[j] - hit).astype(BF16)

    diagonal = lax.broadcasted_iota(jnp.int32, (piece, 128), 0) == lax.broadcasted_iota(
        jnp.int32, (piece, 128), 1
    )

    def narrow_copies(code, got, scale, gots, sems, peers, slot, p):
        rows = pl.ds(slot * c + p * piece, piece)
        line = slot * PIECES + p
        peer = peers[1 << stage_of(slot)]
        return (
            remote(code.at[rows, :], got.at[rows, :], sems[0].at[slot, p], sems[1].at[slot, p], peer),
            remote(scale.at[line], gots.at[line], sems[2].at[slot, p], sems[3].at[slot, p], peer),
        )

    nq_copies = functools.partial(
        narrow_copies, codeq, gotq, scaleq, gotsq, (aqs_sem, aqr_sem, cqs_sem, cqr_sem), peer_q
    )
    nd_copies = functools.partial(
        narrow_copies, coded, gotd, scaled, gotsd, (ads_sem, adr_sem, cds_sem, cdr_sem), peer_d
    )

    def wide_copy(slot, p):
        return remote(
            accq.at[pl.ds(place_q(slot) * c + p * piece, piece), :],
            wideq.at[pl.ds((slot - half) * c + p * piece, piece), :],
            aqs_sem.at[slot, p], aqr_sem.at[slot, p], peer_q[half],
        )

    def send(which, slot, p):
        if which == "q" and slot >= half:
            wide_copy(slot, p).start()
            return
        acc, place, code, scale, copies = (
            (accq, place_q, codeq, scaleq, nq_copies) if which == "q"
            else (accd, place_d, coded, scaled, nd_copies)
        )
        value = acc[pl.ds(place(slot) * c + p * piece, piece), :]
        top = jnp.maximum(jnp.max(jnp.abs(value), axis=1, keepdims=True), 1e-30)
        codes = jnp.round(value * (32767.0 / top))
        code[pl.ds(slot * c + p * piece, piece), :] = codes.astype(jnp.int32).astype(jnp.int16)
        scale[slot * PIECES + p] = jnp.sum(
            jnp.where(diagonal, top * (1.0 / 32767.0), 0.0), axis=0, keepdims=True
        )
        for copy in copies(slot, p):
            copy.start()

    def absorb(which, slots):
        for slot in slots:
            into = slot - (1 << stage_of(slot))
            for p in range(PIECES):
                if which == "q" and slot >= half:
                    wide_copy(slot, p).wait_recv()
                    value = wideq[pl.ds((slot - half) * c + p * piece, piece), :]
                else:
                    got, gots, copies = (
                        (gotq, gotsq, nq_copies) if which == "q" else (gotd, gotsd, nd_copies)
                    )
                    for copy in copies(slot, p):
                        copy.wait_recv()
                    scales = jnp.sum(
                        jnp.where(diagonal, gots[slot * PIECES + p], 0.0), axis=1, keepdims=True
                    )
                    codes = got[pl.ds(slot * c + p * piece, piece), :]
                    value = codes.astype(jnp.int32).astype(F32) * scales
                acc, place = (accq, place_q) if which == "q" else (accd, place_d)
                rows = pl.ds(place(into) * c + p * piece, piece)
                acc[rows, :] = acc[rows, :] + value
                if into and stage_of(slot) == stage_of(into) + 1:
                    send(which, into, p)

    def grad_q(slots):
        for slot in slots:
            rows = pl.ds(place_q(slot) * c, pair)
            accq[rows, :] = lax.dot_general(
                wts[:, rows], dall[...], (((0,), (0,)), ((), ())), preferred_element_type=F32
            )
            for p in range(PIECES):
                send("q", slot + half, p)

    def grad_d(slots):
        for slot in slots:
            rows = pl.ds(place_d(slot) * c, pair)
            accd[rows, :] = jnp.dot(wts[rows, :], qall[...], preferred_element_type=F32)
            for p in range(PIECES):
                send("d", slot + nd // 2, p)

    early_q, late_q = falling(half, half // 2), falling(half // 2, 0)
    for slot in falling(nd // 2, nd // 4):
        weigh([place_d(slot), place_d(slot) + 1])
        grad_d([slot])
    for slot in falling(nd // 4, 0):
        weigh([place_d(slot), place_d(slot) + 1])
    grad_q(early_q)
    absorb("q", [early_q[0] + half])
    grad_d(falling(nd // 4, 0))
    absorb("q", [slot + half for slot in early_q[1:]])
    grad_q(late_q)
    for copy in loss_copies:
        copy.start()

    absorb("d", falling(nd, 3 * nd // 4))
    absorb("q", [slot + half for slot in late_q])
    rest_q, rest_d = falling(half, 2), falling(3 * nd // 4, 1)
    absorb("q", rest_q[:1])
    absorb("d", rest_d[:1])
    for p in range(SHARD_PIECES):
        for slot in range(1, nq):
            gq(slot, p).wait_send()
        for slot in range(1, nd):
            gd(slot, p).wait_send()
    for copy in pos_copies + stat_copies:
        copy.wait_send()
    for i in range(1, max(len(rest_q), len(rest_d))):
        absorb("q", rest_q[i:i + 1])
        absorb("d", rest_d[i:min(i + 1, len(rest_d) - 1)])
    absorb("q", [1])

    own = pl.ds(0, c)
    stores = [
        pltpu.make_async_copy(accq.at[own, :], outq_ref, io_sem.at[3]),
        pltpu.make_async_copy(accd.at[own, :], outd_ref, io_sem.at[4]),
    ]
    accq[own, :] = project(20.0 * accq[own, :], *normalize(qown[...]))
    stores[0].start()
    absorb("d", [1])
    accd[own, :] = project(20.0 * accd[own, :], *normalize(down[...]))
    stores[1].start()

    for copy in loss_copies:
        copy.wait_recv()
    row = tree_sum([losses[k] for k in range(nd)])
    loss_ref[...] = jnp.sum(row, axis=1, keepdims=True) / (c * n)

    for p in range(PIECES):
        for slot in range(1, nq):
            for copy in nq_copies(slot, p) if slot < half else (wide_copy(slot, p),):
                copy.wait_send()
        for slot in range(1, nd):
            for copy in nd_copies(slot, p):
                copy.wait_send()
    for copy in loss_copies:
        copy.wait_send()
    for copy in stores:
        copy.wait()


def hand_over(sumq_ref, sumd_ref, outq_ref, outd_ref, stage, sem):
    rows = sumq_ref.shape[0] // 2
    parts = [
        (ref.at[pl.ds(h * rows, rows), :], out.at[pl.ds(h * rows, rows), :])
        for ref, out in ((sumq_ref, outq_ref), (sumd_ref, outd_ref)) for h in range(2)
    ]
    loads = [
        pltpu.make_async_copy(ref, stage.at[i], sem.at[0, i]) for i, (ref, out) in enumerate(parts)
    ]
    stores = [
        pltpu.make_async_copy(stage.at[i], out, sem.at[1, i]) for i, (ref, out) in enumerate(parts)
    ]
    for copy in loads:
        copy.start()
    for load, store in zip(loads, stores):
        load.wait()
        store.start()
    for copy in stores:
        copy.wait()


def local(queries, documents, positives):
    n = lax.axis_size("dp")
    c, width = queries.shape
    qbits, dbits = group_bits(n)
    nq, nd = 1 << len(qbits), 1 << len(dbits)
    dma = pltpu.SemaphoreType.DMA
    vmem = pl.BlockSpec(memory_space=pltpu.VMEM)
    tile = jax.ShapeDtypeStruct((c, width), F32)
    anywhere = pl.BlockSpec(memory_space=pl.ANY)
    buffers = [
        ((c, width), BF16),
        ((c, width), BF16),
        ((nq * c, width), BF16),
        ((nd * c, width), BF16),
        ((1, nq * c), jnp.int32),
        ((nd * c, nq * c), F32),
        ((nd * c, nq * c), BF16),
        ((nq, 2, nq * c), F32),
        ((nd, 1, c), F32),
        ((nq * c, width), F32),
        ((nd * c, width), F32),
        ((nq // 2 * c, width), F32),
        ((nq // 2 * c, width), jnp.int16),
        ((nq // 2 * c, width), jnp.int16),
        ((nd * c, width), jnp.int16),
        ((nd * c, width), jnp.int16),
        ((nq // 2 * PIECES, 1, 128), F32),
        ((nq // 2 * PIECES, 1, 128), F32),
        ((nd * PIECES, 1, 128), F32),
        ((nd * PIECES, 1, 128), F32),
    ]
    loss, grad_q, grad_d = pl.pallas_call(
        functools.partial(kernel, n, qbits, dbits),
        out_shape=(jax.ShapeDtypeStruct((1, 1), F32), tile, tile),
        in_specs=[anywhere] * 3,
        out_specs=(vmem, anywhere, anywhere),
        scratch_shapes=[pltpu.VMEM(shape, kind) for shape, kind in buffers] + [
            dma((nq, SHARD_PIECES)), dma((nq, SHARD_PIECES)),
            dma((nd, SHARD_PIECES)), dma((nd, SHARD_PIECES)),
            dma((nq,)), dma((nq,)), dma((nq,)), dma((nq,)), dma((nd,)), dma((nd,)),
            dma((nq, PIECES)), dma((nq, PIECES)), dma((nd, PIECES)), dma((nd, PIECES)),
            dma((nq, PIECES)), dma((nq, PIECES)), dma((nd, PIECES)), dma((nd, PIECES)),
            dma((5,)),
        ],
        compiler_params=pltpu.CompilerParams(
            collective_id=0, has_side_effects=True,
            vmem_limit_bytes=VMEM_BYTES,
        ),
        cost_estimate=pl.CostEstimate(
            flops=6 * nq * c * nd * c * width,
            bytes_accessed=12 * c * width,
            transcendentals=nq * c * nd * c,
        ),
    )(queries, documents, positives.reshape(1, c))
    grad_q, grad_d = pl.pallas_call(
        hand_over,
        out_shape=(tile, tile),
        in_specs=[anywhere] * 2,
        out_specs=(anywhere, anywhere),
        scratch_shapes=[pltpu.VMEM((4, c // 2, width), F32), dma((2, 4))],
        compiler_params=pltpu.CompilerParams(vmem_limit_bytes=VMEM_BYTES),
        cost_estimate=pl.CostEstimate(
            flops=0, bytes_accessed=16 * c * width, transcendentals=0
        ),
    )(grad_q, grad_d)
    return (loss.reshape(()), grad_q, grad_d)


def solution(mesh):
    placed = (P("dp", None), P("dp", None), P("dp"))
    return jax.shard_map(
        local,
        mesh=mesh,
        in_specs=placed,
        out_specs=(P(), P("dp", None), P("dp", None)),
        check_vma=False,
    )
```

```python
import functools

import jax
import jax.numpy as jnp
from jax import lax
from jax.experimental import pallas as pl
from jax.experimental.pallas import tpu as pltpu
from jax.sharding import PartitionSpec as P

PIECES = 2
SHARD_PIECES = 4
VMEM_BYTES = 56 << 20
F32 = jnp.float32
BF16 = jnp.bfloat16


def tree_sum(terms):
    while len(terms) > 1:
        terms = [terms[i] + terms[i + 1] for i in range(0, len(terms), 2)]
    return terms[0]


def normalize(values):
    wide = values.astype(F32)
    length = jnp.sqrt(jnp.sum(wide * wide, axis=1, keepdims=True) + 1e-06)
    return wide / length, length


def project(grad, unit, length):
    return (grad - jnp.sum(grad * unit, axis=1, keepdims=True) * unit) / length


def group_bits(n):
    bits = n.bit_length() - 1
    odd = [b for b in range(bits - 1, 0, -1) if b % 2 == 1]
    even = [b for b in range(bits - 1, 0, -1) if b % 2 == 0]
    return odd + [0], even


def stage_of(slot):
    return slot.bit_length() - 1


def place_of(slot, bits):
    return sum(((slot >> j) & 1) << (len(bits) - 1 - j) for j in range(len(bits)))


def falling(high, low):
    return list(range(high - 1, low - 1, -1))


def kernel(
    n, qbits, dbits,
    q_ref, d_ref, pos_ref,
    loss_ref, outq_ref, outd_ref,
    qown, down, qall, dall, posrow, expd, wts, stats, losses, accq, accd, wideq,
    codeq, gotq, coded, gotd, scaleq, gotsq, scaled, gotsd,
    qs_sem, qr_sem, ds_sem, dr_sem, ps_sem, pr_sem, ss_sem, sr_sem, ls_sem, lr_sem,
    aqs_sem, aqr_sem, ads_sem, adr_sem, cqs_sem, cqr_sem, cds_sem, cdr_sem, io_sem,
):
    me = lax.axis_index("dp")
    c, width = q_ref.shape
    piece, part = c // PIECES, c // SHARD_PIECES
    nq, nd = 1 << len(qbits), 1 << len(dbits)
    half = nq // 2

    def flipped(bits, slot):
        where = me
        for j, b in enumerate(bits):
            if (slot >> j) & 1:
                where = where + (1 - 2 * (lax.rem(lax.div(me, 1 << b), 2))) * (1 << b)
        return where

    def place_q(slot):
        return place_of(slot, qbits)

    def place_d(slot):
        return place_of(slot, dbits)

    peer_q = [flipped(qbits, k) for k in range(nq)]
    peer_d = [flipped(dbits, k) for k in range(nd)]

    loads = [
        pltpu.make_async_copy(q_ref, qown, io_sem.at[0]),
        pltpu.make_async_copy(d_ref, down, io_sem.at[1]),
        pltpu.make_async_copy(pos_ref, posrow.at[:, pl.ds(0, c)], io_sem.at[2]),
    ]
    for copy in loads:
        copy.start()
    barrier = pltpu.get_barrier_semaphore()
    for peer in peer_q[1:] + peer_d[1:]:
        pl.semaphore_signal(barrier, inc=1, device_id=(peer,), device_id_type=pl.DeviceIdType.MESH)

    for copy in loads:
        copy.wait()
    qall[pl.ds(0, c), :] = normalize(qown[...])[0].astype(BF16)
    dall[pl.ds(0, c), :] = normalize(down[...])[0].astype(BF16)

    pl.semaphore_wait(barrier, nq + nd - 2)

    def remote(src, dst, send, recv, peer):
        return pltpu.make_async_remote_copy(
            src_ref=src, dst_ref=dst, send_sem=send, recv_sem=recv,
            device_id=(peer,), device_id_type=pl.DeviceIdType.MESH,
        )

    def gather_copy(buf, place, send, recv, peers, slot, p):
        low = slot - (1 << stage_of(slot))
        return remote(
            buf.at[pl.ds(place(low) * c + p * part, part), :],
            buf.at[pl.ds(place(slot) * c + p * part, part), :],
            send.at[slot, p], recv.at[slot, p], peers[1 << stage_of(slot)],
        )

    gq = functools.partial(gather_copy, qall, place_q, qs_sem, qr_sem, peer_q)
    gd = functools.partial(gather_copy, dall, place_d, ds_sem, dr_sem, peer_d)
    pos_copies = [
        remote(posrow.at[:, pl.ds(0, c)], posrow.at[:, pl.ds(place_q(k) * c, c)],
               ps_sem.at[k], pr_sem.at[k], peer_q[k])
        for k in range(1, nq)
    ]

    for p in range(SHARD_PIECES):
        for j in range(len(qbits)):
            gq(1 << j, p).start()
            if j < len(dbits):
                gd(1 << j, p).start()
    for copy in pos_copies:
        copy.start()

    def arrive(make, bits, slots):
        for slot in slots:
            for p in range(SHARD_PIECES):
                make(slot, p).wait_recv()
                for j in range(stage_of(slot) + 1, len(bits)):
                    make(slot + (1 << j), p).start()

    pair = 2 * c
    bases = [peer_d[place_d(i)] * c for i in range(nd)]

    def hits(j, i):
        start = j * pair if isinstance(j, int) else pl.multiple_of(j * pair, pair)
        return lax.broadcasted_iota(jnp.int32, (c, pair), 0) == posrow[:, pl.ds(start, pair)] - bases[i]

    def score(pairs, first, last):

        def step(j, carry):
            lanes = pl.ds(pl.multiple_of(j * pair, pair), pair)
            if first:
                total, picked = stats[0, 0:1, lanes], stats[0, 1:2, lanes]
            else:
                total, picked = jnp.zeros((1, pair), F32), jnp.zeros((1, pair), F32)
            dots = lax.dot_general(
                dall[pl.ds(first * c, (last - first) * c), :], qall[lanes, :],
                (((1,), (1,)), ((), ())), preferred_element_type=F32,
            )
            for i in range(first, last):
                scores = 20.0 * dots[(i - first) * c:(i - first + 1) * c, :]
                powers = jnp.exp(scores - 20.0)
                expd[pl.ds(i * c, c), lanes] = powers
                total = total + jnp.sum(powers, axis=0, keepdims=True)
                picked = picked + jnp.sum(
                    jnp.where(hits(j, i), scores, 0.0), axis=0, keepdims=True
                )
            stats[0, 0:1, lanes] = total
            stats[0, 1:2, lanes] = picked
            return carry

        lax.fori_loop(pairs[0], pairs[1], step, 0, unroll=True)

    arrive(gq, qbits, [1])
    arrive(gq, qbits, range(2, nq, 2))
    arrive(gd, dbits, range(2, nd, 2))
    for copy in pos_copies:
        copy.wait_recv()
    low, high = nd // 2, 3 * nd // 4
    score((0, nq // 4), 0, low)
    arrive(gd, dbits, [1])
    arrive(gq, qbits, [3])
    arrive(gq, qbits, range(5, nq, 4))
    arrive(gd, dbits, range(5, nd, 4))
    score((nq // 4, 3 * nq // 8), 0, low)
    score((0, 3 * nq // 8), low, high)
    arrive(gq, qbits, range(7, nq, 4))
    score((3 * nq // 8, nq // 2), 0, high)
    arrive(gd, dbits, range(3, nd, 4))
    score((0, nq // 2), high, nd)

    stat_copies = [
        remote(stats.at[0], stats.at[k], ss_sem.at[k], sr_sem.at[k], peer_q[k])
        for k in range(1, nq)
    ]
    for copy in stat_copies:
        copy.start()
    for copy in stat_copies:
        copy.wait_recv()

    def slot_total(row, r):
        return tree_sum(
            [stats[k, row:row + 1, pl.ds(place_q(r ^ k) * c, c)] for k in range(nq)]
        )

    totals = [slot_total(0, r) for r in range(nq)]
    loss_copies = [
        remote(losses.at[0], losses.at[k], ls_sem.at[k], lr_sem.at[k], peer_d[k])
        for k in range(1, nd)
    ]

    inverses = [
        1.0 / jnp.concatenate([totals[place_q(2 * j)], totals[place_q(2 * j + 1)]], axis=1)
        for j in range(nq // 2)
    ]

    def weigh(places):
        for i in places:
            rows = pl.ds(i * c, c)
            for j in range(nq // 2):
                lanes = pl.ds(j * pair, pair)
                hit = jnp.where(hits(j, i), 1.0, 0.0)
                wts[rows, lanes] = (expd[rows, lanes] * inverses[j] - hit).astype(BF16)

    diagonal = lax.broadcasted_iota(jnp.int32, (piece, 128), 0) == lax.broadcasted_iota(
        jnp.int32, (piece, 128), 1
    )

    def narrow_copies(code, got, scale, gots, sems, peers, slot, p):
        rows = pl.ds(slot * c + p * piece, piece)
        line = slot * PIECES + p
        peer = peers[1 << stage_of(slot)]
        return (
            remote(code.at[rows, :], got.at[rows, :], sems[0].at[slot, p], sems[1].at[slot, p], peer),
            remote(scale.at[line], gots.at[line], sems[2].at[slot, p], sems[3].at[slot, p], peer),
        )

    nq_copies = functools.partial(
        narrow_copies, codeq, gotq, scaleq, gotsq, (aqs_sem, aqr_sem, cqs_sem, cqr_sem), peer_q
    )
    nd_copies = functools.partial(
        narrow_copies, coded, gotd, scaled, gotsd, (ads_sem, adr_sem, cds_sem, cdr_sem), peer_d
    )

    def wide_copy(slot, p):
        return remote(
            accq.at[pl.ds(place_q(slot) * c + p * piece, piece), :],
            wideq.at[pl.ds((slot - half) * c + p * piece, piece), :],
            aqs_sem.at[slot, p], aqr_sem.at[slot, p], peer_q[half],
        )

    def send(which, slot, p):
        if which == "q" and slot >= half:
            wide_copy(slot, p).start()
            return
        acc, place, code, scale, copies = (
            (accq, place_q, codeq, scaleq, nq_copies) if which == "q"
            else (accd, place_d, coded, scaled, nd_copies)
        )
        value = acc[pl.ds(place(slot) * c + p * piece, piece), :]
        top = jnp.maximum(jnp.max(jnp.abs(value), axis=1, keepdims=True), 1e-30)
        codes = jnp.round(value * (32767.0 / top))
        code[pl.ds(slot * c + p * piece, piece), :] = codes.astype(jnp.int32).astype(jnp.int16)
        scale[slot * PIECES + p] = jnp.sum(
            jnp.where(diagonal, top * (1.0 / 32767.0), 0.0), axis=0, keepdims=True
        )
        for copy in copies(slot, p):
            copy.start()

    def absorb(which, slots):
        for slot in slots:
            into = slot - (1 << stage_of(slot))
            for p in range(PIECES):
                if which == "q" and slot >= half:
                    wide_copy(slot, p).wait_recv()
                    value = wideq[pl.ds((slot - half) * c + p * piece, piece), :]
                else:
                    got, gots, copies = (
                        (gotq, gotsq, nq_copies) if which == "q" else (gotd, gotsd, nd_copies)
                    )
                    for copy in copies(slot, p):
                        copy.wait_recv()
                    scales = jnp.sum(
                        jnp.where(diagonal, gots[slot * PIECES + p], 0.0), axis=1, keepdims=True
                    )
                    codes = got[pl.ds(slot * c + p * piece, piece), :]
                    value = codes.astype(jnp.int32).astype(F32) * scales
                acc, place = (accq, place_q) if which == "q" else (accd, place_d)
                rows = pl.ds(place(into) * c + p * piece, piece)
                acc[rows, :] = acc[rows, :] + value
                if into and stage_of(slot) == stage_of(into) + 1:
                    send(which, into, p)

    def grad_q(slots):
        for slot in slots:
            rows = pl.ds(place_q(slot) * c, pair)
            accq[rows, :] = lax.dot_general(
                wts[:, rows], dall[...], (((0,), (0,)), ((), ())), preferred_element_type=F32
            )
            for p in range(PIECES):
                send("q", slot + half, p)

    def grad_d(slots):
        for slot in slots:
            rows = pl.ds(place_d(slot) * c, pair)
            accd[rows, :] = jnp.dot(wts[rows, :], qall[...], preferred_element_type=F32)
            for p in range(PIECES):
                send("d", slot + nd // 2, p)

    early_q, late_q = falling(half, half // 2), falling(half // 2, 0)
    for slot in falling(nd // 2, nd // 4):
        weigh([place_d(slot), place_d(slot) + 1])
        grad_d([slot])
    for slot in falling(nd // 4, 0):
        weigh([place_d(slot), place_d(slot) + 1])
    grad_q(early_q)
    absorb("q", [early_q[0] + half])
    grad_d(falling(nd // 4, 0))
    absorb("q", [slot + half for slot in early_q[1:]])
    grad_q(late_q)
    losses[0] = tree_sum([20.0 + jnp.log(totals[r]) - slot_total(1, r) for r in range(nq)])
    for copy in loss_copies:
        copy.start()

    absorb("d", falling(nd, 3 * nd // 4))
    absorb("q", [slot + half for slot in late_q])
    rest_q, rest_d = falling(half, 1), falling(3 * nd // 4, 1)
    for i in range(max(len(rest_q), len(rest_d))):
        absorb("q", rest_q[i:i + 1])
        absorb("d", rest_d[i:i + 1])

    own = pl.ds(0, c)
    stores = [
        pltpu.make_async_copy(accq.at[own, :], outq_ref, io_sem.at[3]),
        pltpu.make_async_copy(accd.at[own, :], outd_ref, io_sem.at[4]),
    ]
    accq[own, :] = project(20.0 * accq[own, :], *normalize(qown[...]))
    stores[0].start()
    accd[own, :] = project(20.0 * accd[own, :], *normalize(down[...]))
    stores[1].start()

    for copy in loss_copies:
        copy.wait_recv()
    row = tree_sum([losses[k] for k in range(nd)])
    loss_ref[...] = jnp.sum(row, axis=1, keepdims=True) / (c * n)

    for p in range(SHARD_PIECES):
        for slot in range(1, nq):
            gq(slot, p).wait_send()
        for slot in range(1, nd):
            gd(slot, p).wait_send()
    for p in range(PIECES):
        for slot in range(1, nq):
            for copy in nq_copies(slot, p) if slot < half else (wide_copy(slot, p),):
                copy.wait_send()
        for slot in range(1, nd):
            for copy in nd_copies(slot, p):
                copy.wait_send()
    for copy in pos_copies + stat_copies + loss_copies:
        copy.wait_send()
    for copy in stores:
        copy.wait()


def hand_over(sumq_ref, sumd_ref, outq_ref, outd_ref, stage, sem):
    rows = sumq_ref.shape[0] // 2
    parts = [
        (ref.at[pl.ds(h * rows, rows), :], out.at[pl.ds(h * rows, rows), :])
        for ref, out in ((sumq_ref, outq_ref), (sumd_ref, outd_ref)) for h in range(2)
    ]
    loads = [
        pltpu.make_async_copy(ref, stage.at[i], sem.at[0, i]) for i, (ref, out) in enumerate(parts)
    ]
    stores = [
        pltpu.make_async_copy(stage.at[i], out, sem.at[1, i]) for i, (ref, out) in enumerate(parts)
    ]
    for copy in loads:
        copy.start()
    for load, store in zip(loads, stores):
        load.wait()
        store.start()
    for copy in stores:
        copy.wait()


def local(queries, documents, positives):
    n = lax.axis_size("dp")
    c, width = queries.shape
    qbits, dbits = group_bits(n)
    nq, nd = 1 << len(qbits), 1 << len(dbits)
    dma = pltpu.SemaphoreType.DMA
    vmem = pl.BlockSpec(memory_space=pltpu.VMEM)
    tile = jax.ShapeDtypeStruct((c, width), F32)
    anywhere = pl.BlockSpec(memory_space=pl.ANY)
    buffers = [
        ((c, width), BF16),
        ((c, width), BF16),
        ((nq * c, width), BF16),
        ((nd * c, width), BF16),
        ((1, nq * c), jnp.int32),
        ((nd * c, nq * c), F32),
        ((nd * c, nq * c), BF16),
        ((nq, 2, nq * c), F32),
        ((nd, 1, c), F32),
        ((nq * c, width), F32),
        ((nd * c, width), F32),
        ((nq // 2 * c, width), F32),
        ((nq // 2 * c, width), jnp.int16),
        ((nq // 2 * c, width), jnp.int16),
        ((nd * c, width), jnp.int16),
        ((nd * c, width), jnp.int16),
        ((nq // 2 * PIECES, 1, 128), F32),
        ((nq // 2 * PIECES, 1, 128), F32),
        ((nd * PIECES, 1, 128), F32),
        ((nd * PIECES, 1, 128), F32),
    ]
    loss, grad_q, grad_d = pl.pallas_call(
        functools.partial(kernel, n, qbits, dbits),
        out_shape=(jax.ShapeDtypeStruct((1, 1), F32), tile, tile),
        in_specs=[anywhere] * 3,
        out_specs=(vmem, anywhere, anywhere),
        scratch_shapes=[pltpu.VMEM(shape, kind) for shape, kind in buffers] + [
            dma((nq, SHARD_PIECES)), dma((nq, SHARD_PIECES)),
            dma((nd, SHARD_PIECES)), dma((nd, SHARD_PIECES)),
            dma((nq,)), dma((nq,)), dma((nq,)), dma((nq,)), dma((nd,)), dma((nd,)),
            dma((nq, PIECES)), dma((nq, PIECES)), dma((nd, PIECES)), dma((nd, PIECES)),
            dma((nq, PIECES)), dma((nq, PIECES)), dma((nd, PIECES)), dma((nd, PIECES)),
            dma((5,)),
        ],
        compiler_params=pltpu.CompilerParams(
            collective_id=0, has_side_effects=True,
            vmem_limit_bytes=VMEM_BYTES,
        ),
        cost_estimate=pl.CostEstimate(
            flops=6 * nq * c * nd * c * width,
            bytes_accessed=12 * c * width,
            transcendentals=nq * c * nd * c,
        ),
    )(queries, documents, positives.reshape(1, c))
    grad_q, grad_d = pl.pallas_call(
        hand_over,
        out_shape=(tile, tile),
        in_specs=[anywhere] * 2,
        out_specs=(anywhere, anywhere),
        scratch_shapes=[pltpu.VMEM((4, c // 2, width), F32), dma((2, 4))],
        compiler_params=pltpu.CompilerParams(vmem_limit_bytes=VMEM_BYTES),
        cost_estimate=pl.CostEstimate(
            flops=0, bytes_accessed=16 * c * width, transcendentals=0
        ),
    )(grad_q, grad_d)
    return (loss.reshape(()), grad_q, grad_d)


def solution(mesh):
    placed = (P("dp", None), P("dp", None), P("dp"))
    return jax.shard_map(
        local,
        mesh=mesh,
        in_specs=placed,
        out_specs=(P(), P("dp", None), P("dp", None)),
        check_vma=False,
    )
```
